32 devices in a mesh: leaf: 4 (over z), row: 2 (over core), col: 4 (over y, x).
Axes of the slice: x: 2, y: 2, z: 4, core: 2. Of those that a mesh axis runs over, the one named last changes fastest.
Arguments:
- front_tiles: bfloat16 [4, 8, 4, 2, 128, 8, 4, 2, 128], P('leaf', None, None, 'row', None, None, 'col'), as said below
- regular: float32 [4, 8, 4, 2, 128], P('leaf', None, 'col', 'row'), may hold values from 0.25 to 2.5
- child_map: int32 [4, 62], P('leaf'), may hold values from 0 to 63, as said below
Outputs:
- panel_factor: float32 [4, 8, 4, 2, 128, 256], P('leaf', None, None, 'row', None, 'col')
- parent_update: float32 [4, 4, 4, 2, 128, 8, 4, 2, 128], P('leaf', None, None, 'row', None, None, 'col')
The draws below stay inside these ranges and needn't reach their ends.
Inputs may be any that keep to these rules, and one draw needn't show every extreme that they name: Each leaf's front_tiles form a symmetric positive semidefinite matrix, the product of a block-sparse constraint matrix (2 of 16 variable blocks per block row), a positive diagonal and its transpose; blocks that share no variable block are zero. `child_map`: within a leaf the entries are strictly increasing.
All inputs are finite; a program needn't handle non-finite values.
Results may differ from the reference program's by a relative error of at most 0.0016.
Values may be sent and summed in bfloat16 or wider, within the bound.
No kernel may reach another device: no remote copies, remote signals or barrier semaphores. Data moves between devices by JAX's collectives and lax.ppermute only.
A program may use at most 128 MiB of HBM per device.

```python
import math
import jax
import jax.numpy as jnp
from jax import lax

TILE = 128
NB = 64
NR = 2
VB = 16
LBO = 8
PB = 2
NCB = 62
N_LEAF = 4
N_ROW = 2
N_COL = 4


def draw_front_tiles(key, part):
    order_full = NB * TILE
    value_top = 16
    exp_low = -2
    exp_high = 3
    energy = 85.0
    scale_factor = 1.0 / (energy * NR * TILE)

    def one_front(leaf_key):
        key_ids, key_vals, key_diag = jax.random.split(leaf_key, 3)
        scores = jax.random.randint(key_ids, (NB, VB), 0, 1 << 20) * VB + jnp.arange(VB, dtype=jnp.int32)[None, :]
        chosen_ids = lax.top_k(scores, NR)[1].astype(jnp.int32)
        values = jax.random.randint(key_vals, (NB, NR, TILE, TILE), 1 - value_top, value_top).astype(jnp.float32)
        weights = jnp.exp2(jax.random.randint(key_diag, (VB, TILE), exp_low, exp_high).astype(jnp.float32))
        dense_rows = jnp.zeros((NB, TILE, VB, TILE), jnp.float32)
        dense_rows = dense_rows.at[jnp.arange(NB, dtype=jnp.int32)[:, None], :, chosen_ids, :].set(values)
        scaled = values * weights[chosen_ids][:, :, None, :]

        def one_row(pair_args):
            tiles_row, ids_row = pair_args
            picked = jnp.take(dense_rows, ids_row, axis=2)
            return jnp.einsum('atx,jyax->tjy', tiles_row, picked, precision=lax.Precision.HIGHEST).reshape(TILE, order_full)
        rows_all = lax.map(one_row, (scaled, chosen_ids)).reshape(order_full, order_full)
        return (rows_all * scale_factor).astype(jnp.bfloat16)
    leaf_keys = jax.random.split(jax.random.fold_in(key, 11), N_LEAF)
    fronts = lax.map(one_front, leaf_keys)
    return fronts.reshape(N_LEAF, LBO, N_COL, N_ROW, TILE, LBO, N_COL, N_ROW, TILE)


def draw_child_map(key, part):
    leaf_keys = jax.random.split(jax.random.fold_in(key, 23), N_LEAF)

    def one_map(map_key):
        order = jax.random.permutation(map_key, NB).astype(jnp.int32)
        keep = order < NCB
        ranks = jnp.cumsum(keep.astype(jnp.int32)) - 1
        slots = jnp.where(keep, ranks, NCB).astype(jnp.int32)
        return jnp.zeros((NCB,), jnp.int32).at[slots].set(jnp.arange(NB, dtype=jnp.int32), mode='drop')
    return jax.vmap(one_map)(leaf_keys).astype(jnp.int32)


def level_of(own_key, extent, cuts, least, high):
    factor_of = 1.0
    for axis_at, shards_of in cuts:
        steps = jax.random.uniform(jax.random.fold_in(jax.random.fold_in(own_key, 6), axis_at), (shards_of,), jnp.float32, least / len(cuts), high / len(cuts))
        factor_of = factor_of * jnp.repeat(jnp.exp(steps), extent[axis_at] // shards_of).reshape((-1,) + (1,) * (len(extent) - 1 - axis_at))
    return factor_of


def setup_inputs(seed: int = 0) -> dict:
    streams_of = jax.random.split(jax.random.key(seed), 4)
    front_tiles = draw_front_tiles(jax.random.fold_in(streams_of[3], 71), 0)
    regular = jnp.clip(jnp.exp(math.log(2.5) - 2.3025851 * jax.random.uniform(streams_of[1], (N_LEAF, LBO, N_COL, N_ROW, TILE), jnp.float32) ** level_of(streams_of[1], (N_LEAF, LBO, N_COL, N_ROW, TILE), ((0, 4), (2, 4), (3, 2)), -0.2, 0.2)), 0.25, 2.5)
    child_map = draw_child_map(jax.random.fold_in(streams_of[3], 71), 0)
    return dict(front_tiles=front_tiles, regular=regular, child_map=child_map)


def reference(front_tiles, regular, child_map):
    order_full = NB * TILE
    panel_cols = PB * TILE
    half_outer = LBO // 2
    factors = []
    parents = []
    for pair_id in range(N_LEAF // 2):
        parent_sum = jnp.zeros((NB, TILE, NB, TILE), jnp.float32)
        for leaf_id in (2 * pair_id, 2 * pair_id + 1):
            front_full = front_tiles[leaf_id].reshape(order_full, order_full).astype(jnp.float32)
            front_full = front_full + jnp.diag(regular[leaf_id].reshape(order_full))
            top_factor = jnp.linalg.cholesky(front_full[:panel_cols, :panel_cols])
            lower_rows = jax.scipy.linalg.solve_triangular(top_factor, front_full[panel_cols:, :panel_cols].T, lower=True).T
            factors.append(jnp.concatenate([top_factor, lower_rows], axis=0).reshape(LBO, N_COL, N_ROW, TILE, panel_cols))
            schur_rest = front_full[panel_cols:, panel_cols:] - jnp.dot(lower_rows, lower_rows.T, precision=lax.Precision.HIGHEST)
            rounded = lax.optimization_barrier(schur_rest.astype(jnp.bfloat16)).astype(jnp.float32)
            child_tiles = jnp.transpose(rounded.reshape(NCB, TILE, NCB, TILE), (0, 2, 1, 3))
            targets = child_map[leaf_id].astype(jnp.int32)
            parent_sum = parent_sum.at[targets[:, None], :, targets[None, :], :].add(child_tiles)
        parent_sum = parent_sum.reshape(LBO, N_COL, N_ROW, TILE, LBO, N_COL, N_ROW, TILE)
        parents.append(parent_sum[:half_outer])
        parents.append(parent_sum[half_outer:])
    return (jnp.stack(factors), jnp.stack(parents))
```

```python
import functools

import jax
import jax.numpy as jnp
from jax import lax
from jax.experimental import pallas as pl
from jax.experimental.pallas import tpu as pltpu
from jax.sharding import PartitionSpec as P

NPAN = 1
VMEM_LIMIT = 60 * 1024 * 1024
CLASSES = 5
f32 = jnp.float32
bf16 = jnp.bfloat16
i32 = jnp.int32
HIGHEST = lax.Precision.HIGHEST


def untangle_kernel(tile, ncols, x_ref, out_ref, wide):
    wide[...] = x_ref[...].astype(f32)
    for j in range(ncols):
        out_ref[j] = wide[pl.ds(j, tile, stride=ncols), :].astype(bf16)


def untangled(x, tile, ncols):
    count = x.shape[0] // (tile * ncols)
    return pl.pallas_call(
        functools.partial(untangle_kernel, tile, ncols),
        out_shape=jax.ShapeDtypeStruct((count, ncols, tile, tile), bf16),
        scratch_shapes=[pltpu.VMEM((tile * ncols, tile), f32)],
        grid=(count,),
        in_specs=[pl.BlockSpec((tile * ncols, tile), lambda i: (i, 0))],
        out_specs=pl.BlockSpec((None, ncols, tile, tile), lambda i: (i, 0, 0, 0)),
        name="untangle",
    )(x)


def sort_kernel(dims, parent_ref, where_ref, x_ref, *rest):
    tile, nrows, ncols, rows, cols, cap = dims
    bufs = rest[:CLASSES]
    metas = rest[CLASSES : 2 * CLASSES]
    over_ref = rest[2 * CLASSES]
    wide, blocks, seen, found_v, found, counts, sem, found_sem = rest[2 * CLASSES + 1 :]
    step = pl.program_id(0)
    wide[...] = x_ref[...].astype(f32)
    for j in range(ncols):
        block = wide[pl.ds(j, tile, stride=ncols), :]
        at = step * ncols + j
        blocks[at] = block.astype(bf16)
        top = jnp.max(jnp.abs(block), axis=0, keepdims=True)
        seen[pl.ds(at, 1), :] = jnp.where(top > 0, 1.0, 0.0)

    @pl.when(step == nrows - 1)
    def _():
        hits = lax.dot_general(
            jnp.ones((8, tile), f32),
            seen[...],
            (((1,), (1,)), ((), ())),
            preferred_element_type=f32,
        )
        found_v[...] = hits.astype(i32)
        copy = pltpu.make_async_copy(found_v, found, found_sem)
        copy.start()
        side = where_ref[0]
        row_at = where_ref[1]
        col_at = where_ref[2]
        half = nrows * rows // 2
        for k in range(CLASSES):
            counts[k] = 0
        copy.wait()

        def one_row(i, carry):
            parent_row = parent_ref[i * rows + row_at]

            @pl.when(parent_row >= 0)
            def _():
                moves_leaf = parent_row // half != side
                target_row = parent_row % rows
                moves_row = target_row != row_at
                place_row = parent_row // rows % (nrows // 2)

                def one_col(j, inner):
                    source_col = ((j // rows) * cols + col_at) * rows + j % rows
                    parent_col = parent_ref[source_col]

                    @pl.when((found[0, i * ncols + j] > 0) & (parent_col >= 0))
                    def _():
                        moves_col = parent_col // rows % cols != col_at
                        place_col = parent_col // (rows * cols) * rows + parent_col % rows
                        kind = jnp.where(
                            moves_leaf,
                            jnp.where(moves_col, 4, 3),
                            jnp.where(moves_col, 2, jnp.where(moves_row, 1, 0)),
                        )
                        slot = counts[kind]
                        counts[kind] = slot + 1
                        code = (place_row * ncols + place_col) * rows + target_row
                        for k in range(CLASSES):

                            @pl.when((kind == k) & (slot < cap))
                            def _():
                                metas[k][1 + slot] = code
                                pltpu.make_async_copy(
                                    blocks.at[i * ncols + j], bufs[k].at[slot], sem
                                ).start()

                    return inner

                lax.fori_loop(0, ncols, one_col, 0)

            return carry

        lax.fori_loop(0, nrows, one_row, 0)
        sent = 0
        over = 0
        for k in range(CLASSES):
            taken = jnp.minimum(counts[k], cap)
            metas[k][0] = taken
            sent = sent + taken
            over = over + (counts[k] - taken)
        over_ref[0] = over

        def drain(_, carry):
            pltpu.make_async_copy(blocks.at[0], bufs[0].at[0], sem).wait()
            return carry

        lax.fori_loop(0, sent, drain, 0)


def sorted_blocks(x, parent, where, dims):
    tile, nrows, ncols, rows, cols, cap = dims
    count = nrows * ncols
    smem = pl.BlockSpec(memory_space=pltpu.SMEM)
    return pl.pallas_call(
        functools.partial(sort_kernel, dims),
        out_shape=[jax.ShapeDtypeStruct((cap, tile, tile), bf16)] * CLASSES
        + [jax.ShapeDtypeStruct((cap + 8,), i32)] * CLASSES
        + [jax.ShapeDtypeStruct((1,), i32)],
        grid=(nrows,),
        in_specs=[smem, smem, pl.BlockSpec((tile * ncols, tile), lambda i: (i, 0))],
        out_specs=[pl.BlockSpec(memory_space=pl.ANY)] * CLASSES + [smem] * (CLASSES + 1),
        scratch_shapes=[
            pltpu.VMEM((tile * ncols, tile), f32),
            pltpu.VMEM((count, tile, tile), bf16),
            pltpu.VMEM((count, tile), f32),
            pltpu.VMEM((8, count), i32),
            pltpu.SMEM((8, count), i32),
            pltpu.SMEM((CLASSES,), i32),
            pltpu.SemaphoreType.DMA,
            pltpu.SemaphoreType.DMA,
        ],
        compiler_params=pltpu.CompilerParams(vmem_limit_bytes=VMEM_LIMIT),
        name="sort_blocks",
    )(parent, where, x)


def eliminate(work, tile):
    rows = lax.broadcasted_iota(i32, (tile, tile), 0)
    lanes = lax.broadcasted_iota(i32, (tile, tile), 1)

    def one(k, carry):
        for leaf in range(2):
            left = work[leaf, :, :tile]
            pivot_row = work[leaf, pl.ds(k, 1), :]
            column = jnp.sum(jnp.where(lanes == k, left, 0.0), axis=1, keepdims=True)
            lane_row = lax.broadcasted_iota(i32, (1, tile), 1)
            pivot = jnp.sum(
                jnp.where(lane_row == k, pivot_row[:, :tile], 0.0), axis=1, keepdims=True
            )
            ratio = jnp.where(rows[:, :1] > k, column / pivot, 0.0)
            work[leaf] = work[leaf] - ratio * pivot_row
        return carry

    lax.fori_loop(0, tile, one, 0)


def full_dot(a, b):
    return jnp.dot(a, b, precision=HIGHEST, preferred_element_type=f32)


def corner_kernel(tile, corner_ref, reg_ref, inverse_ref, upper_ref, work):
    rows = lax.broadcasted_iota(i32, (tile, tile), 0)
    lanes = lax.broadcasted_iota(i32, (tile, tile), 1)
    eye = jnp.where(rows == lanes, 1.0, 0.0).astype(f32)

    def block(leaf, i, j):
        value = corner_ref[i, leaf, j].astype(f32)
        if i == j:
            value = value + jnp.where(rows == lanes, reg_ref[i, leaf], 0.0)
        return value

    def finish(leaf):
        upper = work[leaf, :, :tile]
        unit = work[leaf, :, tile:]
        pivots = jnp.sum(jnp.where(rows == lanes, upper, 0.0), axis=1, keepdims=True)
        scale = 1.0 / jnp.sqrt(pivots)
        return jnp.where(lanes >= rows, upper * scale, 0.0), jnp.where(
            lanes <= rows, unit * scale, 0.0
        )

    for leaf in range(2):
        work[leaf, :, :tile] = block(leaf, 0, 0)
        work[leaf, :, tile:] = eye
    eliminate(work, tile)
    for leaf in range(2):
        upper, inverse = finish(leaf)
        cross = full_dot(inverse, block(leaf, 0, 1))
        upper_ref[leaf, :tile, :tile] = upper
        upper_ref[leaf, :tile, tile:] = cross
        upper_ref[leaf, tile:, :tile] = jnp.zeros((tile, tile), f32)
        inverse_ref[leaf, :tile, :tile] = inverse
        inverse_ref[leaf, :tile, tile:] = jnp.zeros((tile, tile), f32)
        work[leaf, :, :tile] = block(leaf, 1, 1) - full_dot(cross.T, cross)
        work[leaf, :, tile:] = eye
    eliminate(work, tile)
    for leaf in range(2):
        upper, inverse = finish(leaf)
        cross = upper_ref[leaf, :tile, tile:]
        upper_ref[leaf, tile:, tile:] = upper
        inverse_ref[leaf, tile:, tile:] = inverse
        low = full_dot(cross.T, inverse_ref[leaf, :tile, :tile])
        inverse_ref[leaf, tile:, :tile] = -full_dot(inverse, low)


def corner_factors(corner, reg, tile):
    wide = jax.ShapeDtypeStruct((2, 2 * tile, 2 * tile), f32)
    return pl.pallas_call(
        functools.partial(corner_kernel, tile),
        out_shape=[wide, wide],
        scratch_shapes=[pltpu.VMEM((2, tile, 2 * tile), f32)],
        name="corner_factors",
    )(corner, reg)


def split3(x):
    high = x.astype(bf16)
    rest = x - high.astype(f32)
    mid = rest.astype(bf16)
    low = (rest - mid.astype(f32)).astype(bf16)
    return high, mid, low


def solve_kernel(dims, source_ref, where_ref, inverse_ref, upper_ref, panel_ref, *rest):
    tile, nrows, ncols, rows, cols, width = dims
    factor_ref, left_ref, right_ref = rest
    row_at = where_ref[1]
    col_at = where_ref[2]
    half = nrows * rows // 2
    side = where_ref[0]

    def raw(leaf, block):
        at = block // rows % cols
        j = block // (rows * cols) * rows + block % rows
        return jnp.concatenate([panel_ref[s * cols + at, leaf, j] for s in range(rows)], axis=0)

    def dots(pieces, value):
        total = jnp.dot(pieces[0], value, preferred_element_type=f32)
        for piece in pieces[1:]:
            total = total + jnp.dot(piece, value, preferred_element_type=f32)
        return total

    own = split3(inverse_ref[0, pl.ds(pl.multiple_of(col_at * width, width), width), :])

    def factor(i, carry):
        factor_ref[i] = dots(own, raw(0, i * rows + row_at))
        return carry

    lax.fori_loop(1, nrows, factor, 0)
    top = upper_ref[0, pl.ds(pl.multiple_of(col_at * width, width), width), :]
    factor_ref[0] = jnp.where(row_at == 0, top[:, :tile], top[:, tile:])
    for leaf in range(2):
        pieces = split3(inverse_ref[leaf])

        def solved(block):
            value = dots(pieces, raw(leaf, jnp.maximum(block, 0)))
            return jnp.where(block >= 0, value, 0.0)

        for j in range(ncols):
            parent = ((j // rows) * cols + col_at) * rows + j % rows
            value = solved(source_ref[leaf, parent])
            high = value.astype(bf16)
            low = (value - high.astype(f32)).astype(bf16)
            depth = rows * tile
            lanes = pl.ds(j * tile, tile)
            right_ref[leaf, :depth, lanes] = high
            right_ref[leaf, depth : 2 * depth, lanes] = low
            right_ref[leaf, 2 * depth :, lanes] = high

        def left(i, carry):
            parent = side * half + i * rows + row_at
            value = solved(source_ref[leaf, parent]).T
            high = value.astype(bf16)
            low = (value - high.astype(f32)).astype(bf16)
            left_ref[leaf, i] = jnp.concatenate([high, high, low], axis=1)
            return carry

        lax.fori_loop(0, nrows // 2, left, 0)


def solved_panels(source, where, inverse, upper, panel, dims):
    tile, nrows, ncols, rows, cols, width = dims
    smem = pl.BlockSpec(memory_space=pltpu.SMEM)
    vmem = pl.BlockSpec(memory_space=pltpu.VMEM)
    depth = 3 * rows * tile
    return pl.pallas_call(
        functools.partial(solve_kernel, dims),
        out_shape=[
            jax.ShapeDtypeStruct((nrows, width, tile), f32),
            jax.ShapeDtypeStruct((2, nrows // 2, tile, depth), bf16),
            jax.ShapeDtypeStruct((2, depth, ncols * tile), bf16),
        ],
        in_specs=[smem, smem, vmem, vmem, vmem],
        out_specs=[vmem, vmem, vmem],
        compiler_params=pltpu.CompilerParams(vmem_limit_bytes=VMEM_LIMIT),
        name="solve_panels",
    )(source, where, inverse, upper, panel)


def merge_kernel(dims, leaves, source_ref, where_ref, *rest):
    tile, nrows, ncols, rows, cols, group = dims
    count = len(leaves)
    metas = rest[:count]
    bufs = rest[count : 2 * count]
    reg_ref, left_ref, right_ref, out_ref = rest[2 * count : 2 * count + 4]
    table, blocks, totals, sem = rest[2 * count + 4 :]
    step = pl.program_id(0)
    side = where_ref[0]
    row_at = where_ref[1]
    col_at = where_ref[2]
    half = nrows * rows // 2
    per_leaf = nrows // 2 * ncols

    @pl.when(step == 0)
    def _():
        def clear(i, carry):
            table[i] = 0
            return carry

        lax.fori_loop(0, 2 * per_leaf, clear, 0)
        blocks[0] = jnp.zeros((tile, tile), bf16)
        filled = 1
        for k in range(count):

            def place(e, slot):
                code = metas[k][1 + e]
                mine = code % rows == row_at

                @pl.when(mine)
                def _():
                    table[leaves[k] * per_leaf + code // rows] = slot
                    pltpu.make_async_copy(bufs[k].at[e], blocks.at[slot], sem).start()

                return slot + jnp.where(mine, 1, 0)

            filled = lax.fori_loop(0, metas[k][0], place, filled)

        def drain(_, carry):
            pltpu.make_async_copy(bufs[0].at[0], blocks.at[0], sem).wait()
            return carry

        lax.fori_loop(1, filled, drain, 0)

    for leaf in range(2):
        left = left_ref[leaf].reshape(group * tile, left_ref.shape[-1])
        totals[leaf] = jnp.dot(left, right_ref[leaf], preferred_element_type=f32)
    on_diagonal = lax.broadcasted_iota(i32, (tile, tile), 0) == lax.broadcasted_iota(
        i32, (tile, tile), 1
    )
    for g in range(group):
        place_row = step * group + g
        parent = side * half + place_row * rows + row_at

        @pl.when(parent // rows % cols == col_at)
        def _():
            j = parent // (rows * cols) * rows + parent % rows
            lanes = pl.ds(pl.multiple_of(j * tile, tile), tile)
            for leaf in range(2):
                block = source_ref[leaf, parent]

                @pl.when(block >= 0)
                def _():
                    at = (block % rows * cols + block // rows % cols) * 2 + leaf
                    gain = reg_ref[at, pl.ds(block // (rows * cols), 1), :]
                    here = totals[leaf, g * tile : (g + 1) * tile, lanes]
                    totals[leaf, g * tile : (g + 1) * tile, lanes] = here - jnp.where(
                        on_diagonal, gain, 0.0
                    )

        for j in range(ncols):
            parts = []
            for leaf in range(2):
                slot = table[leaf * per_leaf + place_row * ncols + j]
                total = totals[leaf, g * tile : (g + 1) * tile, j * tile : (j + 1) * tile]
                parts.append((blocks[slot].astype(f32) - total).astype(bf16).astype(f32))
            out_ref[pl.ds(g * tile * ncols + j, tile, stride=ncols), :] = parts[0] + parts[1]


def merged_parent(source, where, metas, bufs, leaves, reg, left, right, dims):
    tile, nrows, ncols, rows, cols, group = dims
    count = len(leaves)
    smem = pl.BlockSpec(memory_space=pltpu.SMEM)
    hbm = pl.BlockSpec(memory_space=pl.ANY)
    vmem = pl.BlockSpec(memory_space=pltpu.VMEM)
    depth = left.shape[-1]
    return pl.pallas_call(
        functools.partial(merge_kernel, dims, leaves),
        out_shape=jax.ShapeDtypeStruct((nrows // 2 * tile * ncols, tile), f32),
        grid=(nrows // 2 // group,),
        in_specs=[smem] * (2 + count)
        + [hbm] * count
        + [
            vmem,
            pl.BlockSpec((2, group, tile, depth), lambda i: (0, i, 0, 0)),
            vmem,
        ],
        out_specs=pl.BlockSpec((group * tile * ncols, tile), lambda i: (i, 0)),
        scratch_shapes=[
            pltpu.SMEM((nrows * ncols,), i32),
            pltpu.VMEM((nrows * ncols + 1, tile, tile), bf16),
            pltpu.VMEM((2, group * tile, ncols * tile), f32),
            pltpu.SemaphoreType.DMA,
        ],
        compiler_params=pltpu.CompilerParams(vmem_limit_bytes=VMEM_LIMIT),
        name="merge_parent",
    )(source, where, *metas, *bufs, reg, left, right)


def sparse_sources(child_map, blocks, panel_blocks):
    targets = child_map[:, None, :]
    matches = targets == jnp.arange(blocks, dtype=i32)[None, :, None]
    ids = panel_blocks + jnp.arange(child_map.shape[1], dtype=i32)
    return jnp.sum(jnp.where(matches, ids + 1, 0), axis=2) - 1


def shards(front_tiles, regular, child_map):
    rows = lax.axis_size("row")
    cols = lax.axis_size("col")
    leaves = lax.axis_size("leaf")
    row_at = lax.axis_index("row")
    col_at = lax.axis_index("col")
    side = lax.axis_index("leaf") % 2
    tile = front_tiles.shape[-1]
    outer = front_tiles.shape[1]
    nrows = outer * cols
    ncols = outer * rows
    blocks = nrows * rows
    cap = nrows * ncols * 5 // 32
    width = NPAN * rows * tile // cols
    group = 2
    where = jnp.stack([side, row_at, col_at]).astype(i32)
    flat = front_tiles.reshape(nrows * tile * ncols, tile)
    leaf_pairs = [(i, i ^ 1) for i in range(leaves)]
    col_pairs = [(i, (i - 1) % cols) for i in range(cols)]
    row_pairs = [(i, (i + 1) % rows) for i in range(rows)]
    both_pairs = [
        (i * cols + j, (i ^ 1) * cols + (j - 1) % cols)
        for i in range(leaves)
        for j in range(cols)
    ]

    own_panel = untangled(flat[: tile * ncols], tile, ncols)[0]
    own_small = jnp.concatenate(
        [regular.reshape(-1), child_map.reshape(-1).astype(f32)]
    )
    sib_panel = lax.ppermute(own_panel, "leaf", leaf_pairs)
    sib_small = lax.ppermute(own_small, "leaf", leaf_pairs)
    panel = lax.all_gather(jnp.stack([own_panel, sib_panel]), ("row", "col"))
    gains = jnp.stack([own_small[: outer * tile], sib_small[: outer * tile]])
    reg = lax.all_gather(gains, ("row", "col"))
    reg = reg.reshape(rows * cols, 2, outer, tile)
    maps = jnp.stack([child_map.reshape(-1), sib_small[outer * tile :].astype(i32)])
    source = sparse_sources(maps, blocks, NPAN * rows)

    parent = jnp.concatenate([jnp.full((NPAN * rows,), -1, i32), child_map.reshape(-1)])
    *found, over = sorted_blocks(flat, parent, where, (tile, nrows, ncols, rows, cols, cap))
    kept, row_move, col_move, leaf_move, far_move = found[:CLASSES]
    kept_m, row_m, col_m, leaf_m, far_m = found[CLASSES:]
    over = lax.psum(over, ("leaf", "row", "col"))

    far, far_m = [lax.ppermute(v, ("leaf", "col"), both_pairs) for v in (far_move, far_m)]
    beside, beside_m = [lax.ppermute(v, "leaf", leaf_pairs) for v in (leaf_move, leaf_m)]
    near, near_m = [lax.ppermute(v, "col", col_pairs) for v in (col_move, col_m)]
    across, across_m = [lax.ppermute(v, "row", row_pairs) for v in (row_move, row_m)]
    crossed = [
        [lax.ppermute(v, "row", row_pairs) for v in pair]
        for pair in ((near, near_m), (beside, beside_m), (far, far_m))
    ]
    bufs = [kept, across, near, beside, far] + [pair[0] for pair in crossed]
    metas = [kept_m, across_m, near_m, beside_m, far_m] + [pair[1] for pair in crossed]
    owners = (0, 0, 0, 1, 1, 0, 1, 1)

    corner = panel.reshape(rows, cols, 2, ncols, tile, tile)[:, 0, :, :rows]
    corner_reg = reg.reshape(rows, cols, 2, outer, 1, tile)[:, 0, :, 0]
    inverse, upper = corner_factors(corner, corner_reg, tile)
    factor, left, right = solved_panels(
        source, where, inverse, upper, panel, (tile, nrows, ncols, rows, cols, width)
    )
    reg = reg.reshape(rows * cols * 2, outer, tile)

    def sparse():
        return merged_parent(
            source, where, metas, bufs, owners, reg, left, right,
            (tile, nrows, ncols, rows, cols, group),
        )

    def dense():
        own = untangled(flat, tile, ncols)
        other = lax.ppermute(own, "row", row_pairs)
        places = jnp.arange(ncols, dtype=i32)
        col_source = source[0][((places // rows) * cols + col_at) * rows + places % rows]
        col_index = jnp.maximum(col_source, 0)
        col_index = col_index // (rows * cols) * rows + col_index % rows
        from_next = (col_source // rows % cols != col_at)[None, :, None, None]
        col_present = (col_source >= 0)[None, :, None, None]
        halves = []
        for half in range(2):
            half_rows = half * (nrows // 2) + jnp.arange(nrows // 2, dtype=i32)
            row_source = source[0][half_rows * rows + row_at]
            row_index = jnp.maximum(row_source, 0) // rows
            is_own = (row_source % rows == row_at)[:, None, None, None]
            picked = jnp.where(
                is_own, jnp.take(own, row_index, axis=0), jnp.take(other, row_index, axis=0)
            )
            picked = jnp.where((row_source >= 0)[:, None, None, None], picked, jnp.zeros_like(picked))
            following = lax.ppermute(picked, "col", col_pairs)
            picked = jnp.where(
                from_next,
                jnp.take(following, col_index, axis=1),
                jnp.take(picked, col_index, axis=1),
            )
            picked = jnp.where(col_present, picked, jnp.zeros_like(picked))
            halves.append(picked.reshape(nrows * ncols // 2, tile, tile))
        stays = jnp.where(side == 0, halves[0], halves[1])
        leaves_here = jnp.where(side == 0, halves[1], halves[0])
        arrived = lax.ppermute(leaves_here, "leaf", leaf_pairs)
        every = nrows * ncols // 2
        codes = jnp.arange(every, dtype=i32) * rows + row_at
        codes = jnp.concatenate([jnp.full((1,), every, i32), codes])
        return merged_parent(
            source, where, [codes, codes], [stays, arrived], (0, 1), reg, left, right,
            (tile, nrows, ncols, rows, cols, group),
        )

    merged = lax.cond(over[0] > 0, dense, sparse)
    factor = factor.reshape(1, outer, cols, 1, width, tile).swapaxes(4, 5)
    merged = merged.reshape(1, outer // 2, cols, 1, tile, outer, 1, rows, tile)
    return factor, merged


def solution(mesh):
    return jax.shard_map(
        shards,
        mesh=mesh,
        in_specs=(
            P("leaf", None, None, "row", None, None, "col", None, None),
            P("leaf", None, "col", "row", None),
            P("leaf", None),
        ),
        out_specs=(
            P("leaf", None, None, "row", None, "col"),
            P("leaf", None, None, "row", None, None, "col", None, None),
        ),
        check_vma=False,
    )
```

```python
import functools

import jax
import jax.numpy as jnp
from jax import lax
from jax.experimental import pallas as pl
from jax.experimental.pallas import tpu as pltpu
from jax.sharding import PartitionSpec as P

NPAN = 1
VMEM_LIMIT = 60 * 1024 * 1024
CLASSES = 5
f32 = jnp.float32
bf16 = jnp.bfloat16
i32 = jnp.int32
HIGHEST = lax.Precision.HIGHEST


def untangle_kernel(tile, ncols, x_ref, out_ref, wide):
    wide[...] = x_ref[...].astype(f32)
    for j in range(ncols):
        out_ref[j] = wide[pl.ds(j, tile, stride=ncols), :].astype(bf16)


def untangled(x, tile, ncols):
    count = x.shape[0] // (tile * ncols)
    return pl.pallas_call(
        functools.partial(untangle_kernel, tile, ncols),
        out_shape=jax.ShapeDtypeStruct((count, ncols, tile, tile), bf16),
        scratch_shapes=[pltpu.VMEM((tile * ncols, tile), f32)],
        grid=(count,),
        in_specs=[pl.BlockSpec((tile * ncols, tile), lambda i: (i, 0))],
        out_specs=pl.BlockSpec((None, ncols, tile, tile), lambda i: (i, 0, 0, 0)),
        name="untangle",
    )(x)


def panel_kernel(tile, ncols, outer, x_ref, reg_ref, out_ref, wide):
    wide[...] = x_ref[...].astype(f32)
    for j in range(ncols):
        out_ref[pl.ds(j * tile, tile)] = wide[pl.ds(j, tile, stride=ncols), :].astype(bf16)
    pieces = [piece.astype(f32) for piece in split3(reg_ref[...])]
    pad = out_ref.shape[0] - ncols * tile - 3 * outer
    tail = jnp.concatenate(pieces + [jnp.zeros((pad, tile), f32)], axis=0)
    out_ref[pl.ds(ncols * tile, 3 * outer + pad)] = tail.astype(bf16)


def panel_and_gains(x, reg, tile, ncols):
    outer = reg.shape[0]
    tail = -(-(3 * outer + 1) // 16) * 16
    return pl.pallas_call(
        functools.partial(panel_kernel, tile, ncols, outer),
        out_shape=jax.ShapeDtypeStruct((ncols * tile + tail, tile), bf16),
        scratch_shapes=[pltpu.VMEM((tile * ncols, tile), f32)],
        grid=(1,),
        in_specs=[
            pl.BlockSpec((tile * ncols, tile), lambda i: (0, 0)),
            pl.BlockSpec((outer, tile), lambda i: (0, 0)),
        ],
        out_specs=pl.BlockSpec((ncols * tile + tail, tile), lambda i: (0, 0)),
        name="panel_and_gains",
    )(x, reg)


def flag_kernel(tile, ncols, x_ref, hits_ref, seen):
    step = pl.program_id(0)
    lines = tile * ncols
    group = x_ref.shape[0] // lines
    for g in range(group):
        x = x_ref[g * lines : (g + 1) * lines]
        at = pl.multiple_of((step * group + g) * ncols, ncols)
        if ncols % 16 == 0:
            top = jnp.max(jnp.abs(x).reshape(tile, ncols, tile), axis=0)
            seen[pl.ds(at, ncols)] = top.astype(f32)
        else:
            top = jnp.max(jnp.abs(x.astype(f32)).reshape(tile, ncols, tile), axis=0)
            for j in range(ncols):
                seen[pl.ds(at + j, 1)] = top[j : j + 1]

    @pl.when(step == pl.num_programs(0) - 1)
    def _():
        hits_ref[...] = lax.dot_general(
            jnp.ones((8, tile), f32),
            jnp.where(seen[...] > 0, 1.0, 0.0),
            (((1,), (1,)), ((), ())),
            preferred_element_type=f32,
        )


def block_flags(x, tile, nrows, ncols):
    count = nrows * ncols
    return pl.pallas_call(
        functools.partial(flag_kernel, tile, ncols),
        out_shape=jax.ShapeDtypeStruct((8, count), f32),
        grid=(nrows // 4,),
        in_specs=[pl.BlockSpec((4 * tile * ncols, tile), lambda i: (i, 0))],
        out_specs=pl.BlockSpec((8, count), lambda i: (0, 0)),
        scratch_shapes=[pltpu.VMEM((count, tile), f32)],
        compiler_params=pltpu.CompilerParams(vmem_limit_bytes=VMEM_LIMIT),
        cost_estimate=pl.CostEstimate(flops=0, bytes_accessed=30_000_000, transcendentals=0),
        name="block_flags",
    )(x)


def sort_kernel(dims, entry_ref, x_ref, *rest):
    tile, group, ncols, cap = dims
    bufs = rest[:CLASSES]
    wide, blocks, lists, lists_low, counts, sem = rest[CLASSES:]
    step = pl.program_id(0)
    lines = tile * ncols
    lane = lax.broadcasted_iota(i32, (8, tile), 1)
    sublane = lax.broadcasted_iota(i32, (8, tile), 0)

    @pl.when(step == 0)
    def _():
        lists[...] = jnp.zeros_like(lists)
        for k in range(CLASSES):
            counts[k] = 0

    for g in range(group):
        wide[g] = x_ref[g * lines : (g + 1) * lines].astype(f32)

    def one_row(g, carry):
        for j in range(ncols):
            at = (step * group + g) * ncols + j
            entry = entry_ref[at]

            @pl.when(entry >= 0)
            def _():
                kind = entry % 8
                code = entry // 8
                slot = counts[kind]
                counts[kind] = slot + 1
                blocks[at] = wide[g, pl.ds(j, tile, stride=ncols), :].astype(bf16)
                here = jnp.where(sublane == 0, code // 256, code % 256).astype(f32)
                lists[kind] = jnp.where(lane == slot, here, lists[kind])
                for k in range(CLASSES):

                    @pl.when((kind == k) & (slot < cap))
                    def _():
                        pltpu.make_async_copy(blocks.at[at], bufs[k].at[slot], sem).start()

        return carry

    lax.fori_loop(0, group, one_row, 0)

    @pl.when(step == pl.num_programs(0) - 1)
    def _():
        sent = 0
        for k in range(CLASSES):
            taken = jnp.minimum(counts[k], cap)
            sent = sent + taken
            listed = jnp.where(sublane == 2, taken.astype(f32), lists[k])
            lists_low[k] = jnp.concatenate([listed, listed], axis=0).astype(bf16)
        copies = [
            pltpu.make_async_copy(lists_low.at[k], bufs[k].at[cap, pl.ds(0, 16)], sem)
            for k in range(CLASSES)
        ]
        for copy in copies:
            copy.start()

        def drain(_, carry):
            pltpu.make_async_copy(blocks.at[0], bufs[0].at[0], sem).wait()
            return carry

        lax.fori_loop(0, sent, drain, 0)
        for copy in copies:
            copy.wait()


def sorted_blocks(x, entries, dims):
    tile, nrows, ncols, cap = dims
    group = 4
    smem = pl.BlockSpec(memory_space=pltpu.SMEM)
    return pl.pallas_call(
        functools.partial(sort_kernel, (tile, group, ncols, cap)),
        out_shape=[jax.ShapeDtypeStruct((cap + 1, tile, tile), bf16)] * CLASSES,
        grid=(nrows // group,),
        in_specs=[smem, pl.BlockSpec((group * tile * ncols, tile), lambda i: (i, 0))],
        out_specs=[pl.BlockSpec(memory_space=pl.ANY)] * CLASSES,
        scratch_shapes=[
            pltpu.VMEM((group, tile * ncols, tile), f32),
            pltpu.VMEM((nrows * ncols, tile, tile), bf16),
            pltpu.VMEM((CLASSES, 8, tile), f32),
            pltpu.VMEM((CLASSES, 16, tile), bf16),
            pltpu.SMEM((CLASSES,), i32),
            pltpu.SemaphoreType.DMA,
        ],
        compiler_params=pltpu.CompilerParams(vmem_limit_bytes=VMEM_LIMIT),
        cost_estimate=pl.CostEstimate(flops=0, bytes_accessed=60_000_000, transcendentals=0),
        name="sort_blocks",
    )(entries, x)


def block_moves(own_map, side, row_at, col_at, nrows, ncols, rows, cols):
    parent = jnp.concatenate([jnp.full((NPAN * rows,), -1, i32), own_map])
    at_row = parent.reshape(nrows, rows)
    at_row = jnp.where(row_at == 0, at_row[:, 0], at_row[:, 1])[:, None]
    at_col = parent.reshape(nrows // cols, cols, rows)
    at_col = lax.dynamic_index_in_dim(at_col, col_at, 1, keepdims=False).reshape(1, ncols)
    moves_leaf = at_row // (nrows * rows // 2) != side
    moves_col = at_col // rows % cols != col_at
    moves_row = at_row % rows != row_at
    kind = jnp.where(
        moves_leaf,
        jnp.where(moves_col, 4, 3),
        jnp.where(moves_col, 2, jnp.where(moves_row, 1, 0)),
    )
    place_row = at_row // rows % (nrows // 2)
    place_col = at_col // (rows * cols) * rows + at_col % rows
    code = (place_row * ncols + place_col) * rows + at_row % rows
    return jnp.where((at_row >= 0) & (at_col >= 0), code * 8 + kind, -1).reshape(-1)


def eliminate(work, tile):
    rows = lax.broadcasted_iota(i32, (tile, tile), 0)
    lanes = lax.broadcasted_iota(i32, (tile, tile), 1)

    def one(k, carry):
        for leaf in range(2):
            left = work[leaf, :, :tile]
            pivot_row = work[leaf, pl.ds(k, 1), :]
            column = jnp.sum(jnp.where(lanes == k, left, 0.0), axis=1, keepdims=True)
            lane_row = lax.broadcasted_iota(i32, (1, tile), 1)
            pivot = jnp.sum(
                jnp.where(lane_row == k, pivot_row[:, :tile], 0.0), axis=1, keepdims=True
            )
            ratio = jnp.where(rows[:, :1] > k, column / pivot, 0.0)
            work[leaf] = work[leaf] - ratio * pivot_row
        return carry

    lax.fori_loop(0, tile, one, 0)


def full_dot(a, b):
    return jnp.dot(a, b, precision=HIGHEST, preferred_element_type=f32)


def corner_kernel(
    dims, where_ref, mine_ref, other_ref, inverse_ref, upper_ref, work, tiles, tails, sem
):
    tile, ncols, outer, cols = dims
    row_at = where_ref[1]
    first = lax.rem(cols - where_ref[2], cols)
    tail = tails.shape[2]
    copies = []
    for which, ref in ((0, mine_ref), (1, other_ref)):
        at = row_at if which == 0 else 1 - row_at
        copies.append(
            pltpu.make_async_copy(ref.at[first, :, pl.ds(0, 2 * tile)], tiles.at[at], sem.at[0, which])
        )
        copies.append(
            pltpu.make_async_copy(
                ref.at[first, :, pl.ds(ncols * tile, tail)], tails.at[at], sem.at[1, which]
            )
        )
    for copy in copies:
        copy.start()
    for copy in copies:
        copy.wait()
    rows = lax.broadcasted_iota(i32, (tile, tile), 0)
    lanes = lax.broadcasted_iota(i32, (tile, tile), 1)
    eye = jnp.where(rows == lanes, 1.0, 0.0).astype(f32)

    def block(leaf, i, j):
        value = tiles[i, leaf, j * tile : (j + 1) * tile, :].astype(f32)
        if i == j:
            pieces = tails[i, leaf].astype(f32)
            gain = pieces[:1] + pieces[outer : outer + 1] + pieces[2 * outer : 2 * outer + 1]
            value = value + jnp.where(rows == lanes, gain, 0.0)
        return value

    def finish(leaf):
        upper = work[leaf, :, :tile]
        unit = work[leaf, :, tile:]
        pivots = jnp.sum(jnp.where(rows == lanes, upper, 0.0), axis=1, keepdims=True)
        scale = 1.0 / jnp.sqrt(pivots)
        return jnp.where(lanes >= rows, upper * scale, 0.0), jnp.where(
            lanes <= rows, unit * scale, 0.0
        )

    for leaf in range(2):
        work[leaf, :, :tile] = block(leaf, 0, 0)
        work[leaf, :, tile:] = eye
    eliminate(work, tile)
    for leaf in range(2):
        upper, inverse = finish(leaf)
        cross = full_dot(inverse, block(leaf, 0, 1))
        upper_ref[leaf, :tile, :tile] = upper
        upper_ref[leaf, :tile, tile:] = cross
        upper_ref[leaf, tile:, :tile] = jnp.zeros((tile, tile), f32)
        inverse_ref[leaf, :tile, :tile] = inverse
        inverse_ref[leaf, :tile, tile:] = jnp.zeros((tile, tile), f32)
        work[leaf, :, :tile] = block(leaf, 1, 1) - full_dot(cross.T, cross)
        work[leaf, :, tile:] = eye
    eliminate(work, tile)
    for leaf in range(2):
        upper, inverse = finish(leaf)
        cross = upper_ref[leaf, :tile, tile:]
        upper_ref[leaf, tile:, tile:] = upper
        inverse_ref[leaf, tile:, tile:] = inverse
        low = full_dot(cross.T, inverse_ref[leaf, :tile, :tile])
        inverse_ref[leaf, tile:, :tile] = -full_dot(inverse, low)


def corner_factors(where, mine, other, tile, ncols, outer):
    wide = jax.ShapeDtypeStruct((2, 2 * tile, 2 * tile), f32)
    tail = mine.shape[2] - ncols * tile
    hbm = pl.BlockSpec(memory_space=pl.ANY)
    vmem = pl.BlockSpec(memory_space=pltpu.VMEM)
    return pl.pallas_call(
        functools.partial(corner_kernel, (tile, ncols, outer, mine.shape[0])),
        out_shape=[wide, wide],
        in_specs=[pl.BlockSpec(memory_space=pltpu.SMEM), hbm, hbm],
        out_specs=[vmem, vmem],
        scratch_shapes=[
            pltpu.VMEM((2, tile, 2 * tile), f32),
            pltpu.VMEM((2, 2, 2 * tile, tile), bf16),
            pltpu.VMEM((2, 2, tail, tile), bf16),
            pltpu.SemaphoreType.DMA((2, 2)),
        ],
        cost_estimate=pl.CostEstimate(flops=0, bytes_accessed=200_000_000, transcendentals=0),
        name="corner_factors",
    )(where, mine, other)


def split3(x):
    high = x.astype(bf16)
    rest = x - high.astype(f32)
    mid = rest.astype(bf16)
    low = (rest - mid.astype(f32)).astype(bf16)
    return high, mid, low


def solve_kernel(dims, source_ref, where_ref, inverse_ref, upper_ref, mine_ref, other_ref, *rest):
    tile, nrows, ncols, rows, cols, width = dims
    factor_ref, left_ref, right_ref, gains_ref, panel, sem = rest
    row_at = where_ref[1]
    col_at = where_ref[2]
    outer = ncols // rows
    copies = [
        pltpu.make_async_copy(ref.at[k], panel.at[place, lax.rem(col_at + k, cols)], sem)
        for ref, place in ((mine_ref, row_at), (other_ref, 1 - row_at))
        for k in range(cols)
    ]
    for copy in copies:
        copy.start()
    for copy in copies:
        copy.wait()
    for s in range(rows):
        for c in range(cols):
            for leaf in range(2):
                pieces = panel[s, c, leaf, ncols * tile :, :].astype(f32)
                gains_ref[(s * cols + c) * 2 + leaf] = (
                    pieces[:outer] + pieces[outer : 2 * outer] + pieces[2 * outer : 3 * outer]
                )
    col_at = where_ref[2]
    half = nrows * rows // 2
    side = where_ref[0]

    def raw(leaf, block):
        at = block // rows % cols
        j = block // (rows * cols) * rows + block % rows
        lines = pl.ds(pl.multiple_of(j * tile, tile), tile)
        return jnp.concatenate([panel[s, at, leaf, lines, :] for s in range(rows)], axis=0)

    def dots(pieces, value):
        total = jnp.dot(pieces[0], value, preferred_element_type=f32)
        for piece in pieces[1:]:
            total = total + jnp.dot(piece, value, preferred_element_type=f32)
        return total

    own = split3(inverse_ref[0, pl.ds(pl.multiple_of(col_at * width, width), width), :])

    def factor(i, carry):
        factor_ref[i] = dots(own, raw(0, i * rows + row_at))
        return carry

    lax.fori_loop(1, nrows, factor, 0)
    top = upper_ref[0, pl.ds(pl.multiple_of(col_at * width, width), width), :]
    factor_ref[0] = jnp.where(row_at == 0, top[:, :tile], top[:, tile:])
    for leaf in range(2):
        pieces = split3(inverse_ref[leaf])

        def solved(block):
            value = dots(pieces, raw(leaf, jnp.maximum(block, 0)))
            return jnp.where(block >= 0, value, 0.0)

        for j in range(ncols):
            parent = ((j // rows) * cols + col_at) * rows + j % rows
            value = solved(source_ref[leaf, parent])
            high = value.astype(bf16)
            low = (value - high.astype(f32)).astype(bf16)
            depth = rows * tile
            lanes = pl.ds(j * tile, tile)
            right_ref[leaf, :depth, lanes] = high
            right_ref[leaf, depth : 2 * depth, lanes] = low
            right_ref[leaf, 2 * depth :, lanes] = high

        def left(i, carry):
            parent = side * half + i * rows + row_at
            value = solved(source_ref[leaf, parent]).T
            high = value.astype(bf16)
            low = (value - high.astype(f32)).astype(bf16)
            left_ref[leaf, i] = jnp.concatenate([high, high, low], axis=1)
            return carry

        lax.fori_loop(0, nrows // 2, left, 0)


def solved_panels(source, where, inverse, upper, mine, other, dims):
    tile, nrows, ncols, rows, cols, width = dims
    smem = pl.BlockSpec(memory_space=pltpu.SMEM)
    vmem = pl.BlockSpec(memory_space=pltpu.VMEM)
    hbm = pl.BlockSpec(memory_space=pl.ANY)
    depth = 3 * rows * tile
    return pl.pallas_call(
        functools.partial(solve_kernel, dims),
        out_shape=[
            jax.ShapeDtypeStruct((nrows, width, tile), f32),
            jax.ShapeDtypeStruct((2, nrows // 2, tile, depth), bf16),
            jax.ShapeDtypeStruct((2, depth, ncols * tile), bf16),
            jax.ShapeDtypeStruct((rows * cols * 2, ncols // rows, tile), f32),
        ],
        in_specs=[smem, smem, vmem, vmem, hbm, hbm],
        out_specs=[vmem] * 4,
        scratch_shapes=[
            pltpu.VMEM((rows,) + mine.shape, bf16),
            pltpu.SemaphoreType.DMA,
        ],
        compiler_params=pltpu.CompilerParams(vmem_limit_bytes=VMEM_LIMIT),
        cost_estimate=pl.CostEstimate(flops=0, bytes_accessed=100_000_000, transcendentals=0),
        name="solve_panels",
    )(source, where, inverse, upper, mine, other)


def merge_kernel(dims, leaves, source_ref, where_ref, *rest):
    tile, nrows, ncols, rows, cols, group = dims
    count = len(leaves)
    bufs = rest[:count]
    reg_ref, left_ref, right_ref, out_ref = rest[count : count + 4]
    table, blocks, totals, lists_low, lists_v, lists, sem = rest[count + 4 :]
    step = pl.program_id(0)
    side = where_ref[0]
    row_at = where_ref[1]
    col_at = where_ref[2]
    half = nrows * rows // 2
    per_leaf = nrows // 2 * ncols

    @pl.when(step == 0)
    def _():
        def clear(i, carry):
            table[i] = 0
            return carry

        copies = [
            pltpu.make_async_copy(
                bufs[k].at[bufs[k].shape[0] - 1, pl.ds(0, 16)], lists_low.at[k], sem
            )
            for k in range(count)
        ]
        for copy in copies:
            copy.start()
        lax.fori_loop(0, 2 * per_leaf, clear, 0)
        blocks[0] = jnp.zeros((tile, tile), bf16)
        filled = 1
        for copy in copies:
            copy.wait()
        for k in range(count):
            listed = lists_low[k].astype(f32)
            codes = listed[0:1] * 256.0 + listed[1:2]
            lists_v[k] = jnp.concatenate([codes, listed[2:3]] + [codes] * 6, axis=0).astype(i32)
        copy = pltpu.make_async_copy(lists_v, lists, sem)
        copy.start()
        copy.wait()
        for k in range(count):

            def place(e, slot):
                code = lists[k, 0, e]
                mine = code % rows == row_at

                @pl.when(mine)
                def _():
                    table[leaves[k] * per_leaf + code // rows] = slot
                    pltpu.make_async_copy(bufs[k].at[e], blocks.at[slot], sem).start()

                return slot + jnp.where(mine, 1, 0)

            filled = lax.fori_loop(0, lists[k, 1, 0], place, filled)

        def drain(_, carry):
            pltpu.make_async_copy(bufs[0].at[0], blocks.at[0], sem).wait()
            return carry

        lax.fori_loop(1, filled, drain, 0)

    for leaf in range(2):
        left = left_ref[leaf].reshape(group * tile, left_ref.shape[-1])
        totals[leaf] = jnp.dot(left, right_ref[leaf], preferred_element_type=f32)
    on_diagonal = lax.broadcasted_iota(i32, (tile, tile), 0) == lax.broadcasted_iota(
        i32, (tile, tile), 1
    )
    for g in range(group):
        place_row = step * group + g
        parent = side * half + place_row * rows + row_at

        @pl.when(parent // rows % cols == col_at)
        def _():
            j = parent // (rows * cols) * rows + parent % rows
            lanes = pl.ds(pl.multiple_of(j * tile, tile), tile)
            for leaf in range(2):
                block = source_ref[leaf, parent]

                @pl.when(block >= 0)
                def _():
                    at = (block % rows * cols + block // rows % cols) * 2 + leaf
                    gain = reg_ref[at, pl.ds(block // (rows * cols), 1), :]
                    here = totals[leaf, g * tile : (g + 1) * tile, lanes]
                    totals[leaf, g * tile : (g + 1) * tile, lanes] = here - jnp.where(
                        on_diagonal, gain, 0.0
                    )

        for j in range(ncols):
            parts = []
            for leaf in range(2):
                slot = table[leaf * per_leaf + place_row * ncols + j]
                total = totals[leaf, g * tile : (g + 1) * tile, j * tile : (j + 1) * tile]
                parts.append((blocks[slot].astype(f32) - total).astype(bf16).astype(f32))
            out_ref[pl.ds(g * tile * ncols + j, tile, stride=ncols), :] = parts[0] + parts[1]


def merged_parent(source, where, bufs, leaves, reg, left, right, dims):
    tile, nrows, ncols, rows, cols, group = dims
    count = len(leaves)
    smem = pl.BlockSpec(memory_space=pltpu.SMEM)
    hbm = pl.BlockSpec(memory_space=pl.ANY)
    vmem = pl.BlockSpec(memory_space=pltpu.VMEM)
    depth = left.shape[-1]
    return pl.pallas_call(
        functools.partial(merge_kernel, dims, leaves),
        out_shape=jax.ShapeDtypeStruct((nrows // 2 * tile * ncols, tile), f32),
        grid=(nrows // 2 // group,),
        in_specs=[smem] * 2
        + [hbm] * count
        + [
            vmem,
            pl.BlockSpec((2, group, tile, depth), lambda i: (0, i, 0, 0)),
            vmem,
        ],
        out_specs=pl.BlockSpec((group * tile * ncols, tile), lambda i: (i, 0)),
        scratch_shapes=[
            pltpu.SMEM((nrows * ncols,), i32),
            pltpu.VMEM((nrows * ncols + 1, tile, tile), bf16),
            pltpu.VMEM((2, group * tile, ncols * tile), f32),
            pltpu.VMEM((count, 16, tile), bf16),
            pltpu.VMEM((count, 8, tile), i32),
            pltpu.SMEM((count, 8, tile), i32),
            pltpu.SemaphoreType.DMA,
        ],
        compiler_params=pltpu.CompilerParams(vmem_limit_bytes=VMEM_LIMIT),
        name="merge_parent",
    )(source, where, *bufs, reg, left, right)


def sparse_sources(child_map, blocks, panel_blocks):
    targets = child_map[:, None, :]
    matches = targets == jnp.arange(blocks, dtype=i32)[None, :, None]
    ids = panel_blocks + jnp.arange(child_map.shape[1], dtype=i32)
    return jnp.sum(jnp.where(matches, ids + 1, 0), axis=2) - 1


def shards(front_tiles, regular, child_map):
    rows = lax.axis_size("row")
    cols = lax.axis_size("col")
    leaves = lax.axis_size("leaf")
    row_at = lax.axis_index("row")
    col_at = lax.axis_index("col")
    side = lax.axis_index("leaf") % 2
    tile = front_tiles.shape[-1]
    outer = front_tiles.shape[1]
    nrows = outer * cols
    ncols = outer * rows
    blocks = nrows * rows
    cap = nrows * ncols * 5 // 32
    width = NPAN * rows * tile // cols
    group = 2
    where = jnp.stack([side, row_at, col_at]).astype(i32)
    flat = front_tiles.reshape(nrows * tile * ncols, tile)
    leaf_pairs = [(i, i ^ 1) for i in range(leaves)]
    col_pairs = [(i, (i - 1) % cols) for i in range(cols)]
    row_pairs = [(i, (i + 1) % rows) for i in range(rows)]
    both_pairs = [
        (i * cols + j, (i ^ 1) * cols + (j - 1) % cols)
        for i in range(leaves)
        for j in range(cols)
    ]

    def from_each_col(value):
        pairs = [[(j, (j - k) % cols) for j in range(cols)] for k in range(cols)]
        return [value] + [lax.ppermute(value, "col", pairs[k]) for k in range(1, cols)]

    own_panel = panel_and_gains(flat, regular.reshape(outer, tile), tile, ncols)
    own_map = child_map.reshape(-1)
    sib_panel = lax.ppermute(own_panel, "leaf", leaf_pairs)
    sib_map = lax.ppermute(own_map, "leaf", leaf_pairs)
    own_panels = from_each_col(own_panel)
    maps = jnp.stack([own_map, sib_map])
    source = sparse_sources(maps, blocks, NPAN * rows)

    hits = block_flags(flat, tile, nrows, ncols)
    moves = block_moves(own_map, side, row_at, col_at, nrows, ncols, rows, cols)
    entries = jnp.where(hits[0] > 0, moves, -1)
    kinds = jnp.arange(CLASSES, dtype=i32)[:, None]
    counts = jnp.sum(((entries >= 0)[None, :] & (entries % 8 == kinds)).astype(i32), axis=1)
    over = jnp.max(counts, keepdims=True) - cap
    sib_panel, entries, over = lax.optimization_barrier((sib_panel, entries, over))
    over = jnp.maximum(over, lax.ppermute(over, "leaf", leaf_pairs))
    mark = jnp.where(over > 0, 1.0, 0.0).astype(bf16)
    mark_row = own_panel.shape[0] - 1
    sib_panel = lax.dynamic_update_slice(
        sib_panel, jnp.broadcast_to(mark[:, None], (1, tile)), (mark_row, 0)
    )
    sib_panels = from_each_col(sib_panel)
    found = sorted_blocks(flat, entries, (tile, nrows, ncols, cap))
    found, own_panels, sib_panels, source = lax.optimization_barrier(
        (found, own_panels, sib_panels, source)
    )
    kept, row_move, col_move, leaf_move, far_move = found
    far = lax.ppermute(far_move, ("leaf", "col"), both_pairs)
    beside = lax.ppermute(leaf_move, "leaf", leaf_pairs)
    near = lax.ppermute(col_move, "col", col_pairs)
    across = lax.ppermute(row_move, "row", row_pairs)
    mine = jnp.stack([jnp.stack(pair) for pair in zip(own_panels, sib_panels)])
    other = lax.ppermute(mine, "row", row_pairs)
    inverse, upper = corner_factors(where, mine, other, tile, ncols, outer)
    factor, left, right, reg = solved_panels(
        source, where, inverse, upper, mine, other, (tile, nrows, ncols, rows, cols, width)
    )
    marks = jnp.concatenate([mine[:, 1, mark_row, 0], other[:, 1, mark_row, 0]])
    over = jnp.max(marks.astype(f32)) > 0
    near, beside, far, left, right = lax.optimization_barrier((near, beside, far, left, right))
    crossed = [lax.ppermute(v, "row", row_pairs) for v in (near, beside, far)]
    bufs = [kept, across, near, beside, far] + crossed
    owners = (0, 0, 0, 1, 1, 0, 1, 1)

    def sparse():
        return merged_parent(
            source, where, bufs, owners, reg, left, right,
            (tile, nrows, ncols, rows, cols, group),
        )

    def dense():
        own = untangled(flat, tile, ncols)
        other = lax.ppermute(own, "row", row_pairs)
        places = jnp.arange(ncols, dtype=i32)
        col_source = source[0][((places // rows) * cols + col_at) * rows + places % rows]
        col_index = jnp.maximum(col_source, 0)
        col_index = col_index // (rows * cols) * rows + col_index % rows
        from_next = (col_source // rows % cols != col_at)[None, :, None, None]
        col_present = (col_source >= 0)[None, :, None, None]
        halves = []
        for half in range(2):
            half_rows = half * (nrows // 2) + jnp.arange(nrows // 2, dtype=i32)
            row_source = source[0][half_rows * rows + row_at]
            row_index = jnp.maximum(row_source, 0) // rows
            is_own = (row_source % rows == row_at)[:, None, None, None]
            picked = jnp.where(
                is_own, jnp.take(own, row_index, axis=0), jnp.take(other, row_index, axis=0)
            )
            picked = jnp.where((row_source >= 0)[:, None, None, None], picked, jnp.zeros_like(picked))
            following = lax.ppermute(picked, "col", col_pairs)
            picked = jnp.where(
                from_next,
                jnp.take(following, col_index, axis=1),
                jnp.take(picked, col_index, axis=1),
            )
            picked = jnp.where(col_present, picked, jnp.zeros_like(picked))
            halves.append(picked.reshape(nrows * ncols // 2, tile, tile))
        stays = jnp.where(side == 0, halves[0], halves[1])
        leaves_here = jnp.where(side == 0, halves[1], halves[0])
        arrived = lax.ppermute(leaves_here, "leaf", leaf_pairs)
        every = nrows * ncols // 2
        part = min(every, tile)
        bufs = []
        for value in (stays, arrived):
            for first in range(0, every, part):
                codes = (first + jnp.arange(tile, dtype=i32)) * rows + row_at
                listed = jnp.stack([codes // 256, codes % 256, jnp.full((tile,), part, i32)])
                listed = jnp.pad(listed, ((0, tile - 3), (0, 0))).astype(bf16)
                bufs.append(jnp.concatenate([value[first : first + part], listed[None]]))
        owners = (0,) * (len(bufs) // 2) + (1,) * (len(bufs) // 2)
        return merged_parent(
            source, where, bufs, owners, reg, left, right,
            (tile, nrows, ncols, rows, cols, group),
        )

    merged = lax.cond(over, dense, sparse)
    factor = factor.reshape(1, outer, cols, 1, width, tile).swapaxes(4, 5)
    merged = merged.reshape(1, outer // 2, cols, 1, tile, outer, 1, rows, tile)
    return factor, merged


def solution(mesh):
    return jax.shard_map(
        shards,
        mesh=mesh,
        in_specs=(
            P("leaf", None, None, "row", None, None, "col", None, None),
            P("leaf", None, "col", "row", None),
            P("leaf", None),
        ),
        out_specs=(
            P("leaf", None, None, "row", None, "col"),
            P("leaf", None, None, "row", None, None, "col", None, None),
        ),
        check_vma=False,
    )
```

```python
import functools

import jax
import jax.numpy as jnp
from jax import lax
from jax.experimental import pallas as pl
from jax.experimental.pallas import tpu as pltpu
from jax.sharding import PartitionSpec as P

NPAN = 1
VMEM_LIMIT = 60 * 1024 * 1024
PART = 8
f32 = jnp.float32
bf16 = jnp.bfloat16
i32 = jnp.int32
HIGHEST = lax.Precision.HIGHEST


def untangle_kernel(tile, ncols, x_ref, out_ref, wide):
    wide[...] = x_ref[...].astype(f32)
    for j in range(ncols):
        out_ref[j] = wide[pl.ds(j, tile, stride=ncols), :].astype(bf16)


def untangled(x, tile, ncols):
    count = x.shape[0] // (tile * ncols)
    return pl.pallas_call(
        functools.partial(untangle_kernel, tile, ncols),
        out_shape=jax.ShapeDtypeStruct((count, ncols, tile, tile), bf16),
        scratch_shapes=[pltpu.VMEM((tile * ncols, tile), f32)],
        grid=(count,),
        in_specs=[pl.BlockSpec((tile * ncols, tile), lambda i: (i, 0))],
        out_specs=pl.BlockSpec((None, ncols, tile, tile), lambda i: (i, 0, 0, 0)),
        name="untangle",
    )(x)


def panel_kernel(tile, ncols, outer, x_ref, reg_ref, out_ref, wide):
    wide[...] = x_ref[...].astype(f32)
    for j in range(ncols):
        out_ref[pl.ds(j * tile, tile)] = wide[pl.ds(j, tile, stride=ncols), :].astype(bf16)
    pieces = [piece.astype(f32) for piece in split3(reg_ref[...])]
    pad = out_ref.shape[0] - ncols * tile - 3 * outer
    tail = jnp.concatenate(pieces + [jnp.zeros((pad, tile), f32)], axis=0)
    out_ref[pl.ds(ncols * tile, 3 * outer + pad)] = tail.astype(bf16)


def panel_and_gains(x, reg, tile, ncols):
    outer = reg.shape[0]
    tail = -(-(3 * outer + 1) // 16) * 16
    return pl.pallas_call(
        functools.partial(panel_kernel, tile, ncols, outer),
        out_shape=jax.ShapeDtypeStruct((ncols * tile + tail, tile), bf16),
        scratch_shapes=[pltpu.VMEM((tile * ncols, tile), f32)],
        grid=(1,),
        in_specs=[
            pl.BlockSpec((tile * ncols, tile), lambda i: (0, 0)),
            pl.BlockSpec((outer, tile), lambda i: (0, 0)),
        ],
        out_specs=pl.BlockSpec((ncols * tile + tail, tile), lambda i: (0, 0)),
        name="panel_and_gains",
    )(x, reg)


def flag_kernel(tile, ncols, x_ref, hits_ref, seen):
    step = pl.program_id(0)
    lines = tile * ncols
    group = x_ref.shape[0] // lines
    for g in range(group):
        x = x_ref[g * lines : (g + 1) * lines]
        at = pl.multiple_of((step * group + g) * ncols, ncols)
        if ncols % 16 == 0:
            top = jnp.max(jnp.abs(x).reshape(tile, ncols, tile), axis=0)
            seen[pl.ds(at, ncols)] = top.astype(f32)
        else:
            top = jnp.max(jnp.abs(x.astype(f32)).reshape(tile, ncols, tile), axis=0)
            for j in range(ncols):
                seen[pl.ds(at + j, 1)] = top[j : j + 1]

    @pl.when(step == pl.num_programs(0) - 1)
    def _():
        hits_ref[...] = lax.dot_general(
            jnp.ones((8, tile), f32),
            jnp.where(seen[...] > 0, 1.0, 0.0),
            (((1,), (1,)), ((), ())),
            preferred_element_type=f32,
        )


def block_flags(x, tile, nrows, ncols):
    count = nrows * ncols
    return pl.pallas_call(
        functools.partial(flag_kernel, tile, ncols),
        out_shape=jax.ShapeDtypeStruct((8, count), f32),
        grid=(nrows // 8,),
        in_specs=[pl.BlockSpec((8 * tile * ncols, tile), lambda i: (i, 0))],
        out_specs=pl.BlockSpec((8, count), lambda i: (0, 0)),
        scratch_shapes=[pltpu.VMEM((count, tile), f32)],
        compiler_params=pltpu.CompilerParams(vmem_limit_bytes=VMEM_LIMIT),
        cost_estimate=pl.CostEstimate(flops=0, bytes_accessed=30_000_000, transcendentals=0),
        name="block_flags",
    )(x)


def sort_kernel(dims, entry_ref, x_ref, *rest):
    tile, group, ncols, rows, rooms = dims
    regions = len(rooms)
    bufs = rest[:regions]
    wide, blocks, lists, lists_low, counts, sem = rest[regions:]
    step = pl.program_id(0)
    lines = tile * ncols
    lane = lax.broadcasted_iota(i32, (8, tile), 1)
    sublane = lax.broadcasted_iota(i32, (8, tile), 0)

    @pl.when(step == 0)
    def _():
        lists[...] = jnp.zeros_like(lists)
        for k in range(regions * 2):
            counts[k] = 0

    for g in range(group):
        wide[g] = x_ref[g * lines : (g + 1) * lines].astype(f32)

    def one_row(g, carry):
        for j in range(ncols):
            at = (step * group + g) * ncols + j
            entry = entry_ref[at]

            @pl.when(entry >= 0)
            def _():
                kind = entry % 8
                end = entry // 8 % rows
                code = entry // (8 * rows)
                held = counts[kind * 2] + counts[kind * 2 + 1]
                spills = (kind >= 2) & (held >= rooms[2])
                region = jnp.where(spills, kind + 3, kind)
                room = jnp.where(spills, rooms[5], jnp.where(kind >= 2, rooms[2], rooms[0]))
                front = counts[region * 2]
                back = counts[region * 2 + 1]
                slot = jnp.where(end == 0, front, room - 1 - back)

                @pl.when(front + back < room)
                def _():
                    counts[region * 2 + end] = jnp.where(end == 0, front, back) + 1
                    blocks[at] = wide[g, pl.ds(j, tile, stride=ncols), :].astype(bf16)
                    here = jnp.where(sublane == 0, code // 256, code % 256).astype(f32)
                    lists[region] = jnp.where(lane == slot, here, lists[region])
                    for k in range(regions):

                        @pl.when(region == k)
                        def _():
                            pltpu.make_async_copy(blocks.at[at], bufs[k].at[slot], sem).start()

        return carry

    lax.fori_loop(0, group, one_row, 0)

    @pl.when(step == pl.num_programs(0) - 1)
    def _():
        sent = 0
        for k in range(regions):
            front = counts[2 * k]
            back = counts[2 * k + 1]
            sent = sent + front + back
            listed = jnp.where(sublane == 2, front.astype(f32), lists[k])
            listed = jnp.where(sublane == 3, back.astype(f32), listed)
            lists_low[k] = jnp.concatenate([listed, listed], axis=0).astype(bf16)
        copies = [
            pltpu.make_async_copy(lists_low.at[k], bufs[k].at[rooms[k], pl.ds(0, 16)], sem)
            for k in range(regions)
        ]
        for copy in copies:
            copy.start()

        def drain(_, carry):
            pltpu.make_async_copy(blocks.at[0], bufs[0].at[0], sem).wait()
            return carry

        lax.fori_loop(0, sent, drain, 0)
        for copy in copies:
            copy.wait()


def sorted_blocks(x, entries, dims):
    tile, nrows, ncols, rows, rooms = dims
    group = 4
    return pl.pallas_call(
        functools.partial(sort_kernel, (tile, group, ncols, rows, rooms)),
        out_shape=[jax.ShapeDtypeStruct((room + 1, tile, tile), bf16) for room in rooms],
        grid=(nrows // group,),
        in_specs=[
            pl.BlockSpec(memory_space=pltpu.SMEM),
            pl.BlockSpec((group * tile * ncols, tile), lambda i: (i, 0)),
        ],
        out_specs=[pl.BlockSpec(memory_space=pl.ANY)] * len(rooms),
        scratch_shapes=[
            pltpu.VMEM((group, tile * ncols, tile), f32),
            pltpu.VMEM((nrows * ncols, tile, tile), bf16),
            pltpu.VMEM((len(rooms), 8, tile), f32),
            pltpu.VMEM((len(rooms), 16, tile), bf16),
            pltpu.SMEM((len(rooms) * 2,), i32),
            pltpu.SemaphoreType.DMA,
        ],
        compiler_params=pltpu.CompilerParams(vmem_limit_bytes=VMEM_LIMIT),
        cost_estimate=pl.CostEstimate(flops=0, bytes_accessed=60_000_000, transcendentals=0),
        name="sort_blocks",
    )(entries, x)


def block_moves(own_map, side, row_at, col_at, nrows, ncols, rows, cols):
    parent = jnp.concatenate([jnp.full((NPAN * rows,), -1, i32), own_map])
    at_row = parent.reshape(nrows, rows)
    at_row = jnp.where(row_at == 0, at_row[:, 0], at_row[:, 1])[:, None]
    at_col = parent.reshape(nrows // cols, cols, rows)
    at_col = lax.dynamic_index_in_dim(at_col, col_at, 1, keepdims=False).reshape(1, ncols)
    moves_leaf = at_row // (nrows * rows // 2) != side
    moves_col = at_col // rows % cols != col_at
    moves_row = at_row % rows != row_at
    kind = jnp.where(
        moves_leaf,
        jnp.where(moves_col, 4, 3),
        jnp.where(moves_col, 2, jnp.where(moves_row, 1, 0)),
    )
    place_row = at_row // rows % (nrows // 2)
    place_col = at_col // (rows * cols) * rows + at_col % rows
    code = (place_row * ncols + place_col) * rows + at_row % rows
    return jnp.where((at_row >= 0) & (at_col >= 0), code * 8 + kind, -1).reshape(-1)


def eliminate(work, tile):
    rows = lax.broadcasted_iota(i32, (tile, tile), 0)
    lanes = lax.broadcasted_iota(i32, (tile, tile), 1)

    def one(k, carry):
        for leaf in range(2):
            left = work[leaf, :, :tile]
            pivot_row = work[leaf, pl.ds(k, 1), :]
            column = jnp.sum(jnp.where(lanes == k, left, 0.0), axis=1, keepdims=True)
            lane_row = lax.broadcasted_iota(i32, (1, tile), 1)
            pivot = jnp.sum(
                jnp.where(lane_row == k, pivot_row[:, :tile], 0.0), axis=1, keepdims=True
            )
            ratio = jnp.where(rows[:, :1] > k, column / pivot, 0.0)
            work[leaf] = work[leaf] - ratio * pivot_row
        return carry

    lax.fori_loop(0, tile, one, 0)


def full_dot(a, b):
    return jnp.dot(a, b, precision=HIGHEST, preferred_element_type=f32)


def corner_kernel(
    dims, where_ref, mine_ref, other_ref, inverse_ref, upper_ref, work, tiles, tails, sem
):
    tile, ncols, outer, cols = dims
    row_at = where_ref[1]
    first = lax.rem(cols - where_ref[2], cols)
    tail = tails.shape[2]
    copies = []
    for which, ref in ((0, mine_ref), (1, other_ref)):
        at = row_at if which == 0 else 1 - row_at
        copies.append(
            pltpu.make_async_copy(ref.at[first, :, pl.ds(0, 2 * tile)], tiles.at[at], sem.at[0, which])
        )
        copies.append(
            pltpu.make_async_copy(
                ref.at[first, :, pl.ds(ncols * tile, tail)], tails.at[at], sem.at[1, which]
            )
        )
    for copy in copies:
        copy.start()
    for copy in copies:
        copy.wait()
    rows = lax.broadcasted_iota(i32, (tile, tile), 0)
    lanes = lax.broadcasted_iota(i32, (tile, tile), 1)
    eye = jnp.where(rows == lanes, 1.0, 0.0).astype(f32)

    def block(leaf, i, j):
        value = tiles[i, leaf, j * tile : (j + 1) * tile, :].astype(f32)
        if i == j:
            pieces = tails[i, leaf].astype(f32)
            gain = pieces[:1] + pieces[outer : outer + 1] + pieces[2 * outer : 2 * outer + 1]
            value = value + jnp.where(rows == lanes, gain, 0.0)
        return value

    def finish(leaf):
        upper = work[leaf, :, :tile]
        unit = work[leaf, :, tile:]
        pivots = jnp.sum(jnp.where(rows == lanes, upper, 0.0), axis=1, keepdims=True)
        scale = 1.0 / jnp.sqrt(pivots)
        return jnp.where(lanes >= rows, upper * scale, 0.0), jnp.where(
            lanes <= rows, unit * scale, 0.0
        )

    for leaf in range(2):
        work[leaf, :, :tile] = block(leaf, 0, 0)
        work[leaf, :, tile:] = eye
    eliminate(work, tile)
    for leaf in range(2):
        upper, inverse = finish(leaf)
        cross = full_dot(inverse, block(leaf, 0, 1))
        upper_ref[leaf, :tile, :tile] = upper
        upper_ref[leaf, :tile, tile:] = cross
        upper_ref[leaf, tile:, :tile] = jnp.zeros((tile, tile), f32)
        inverse_ref[leaf, :tile, :tile] = inverse
        inverse_ref[leaf, :tile, tile:] = jnp.zeros((tile, tile), f32)
        work[leaf, :, :tile] = block(leaf, 1, 1) - full_dot(cross.T, cross)
        work[leaf, :, tile:] = eye
    eliminate(work, tile)
    for leaf in range(2):
        upper, inverse = finish(leaf)
        cross = upper_ref[leaf, :tile, tile:]
        upper_ref[leaf, tile:, tile:] = upper
        inverse_ref[leaf, tile:, tile:] = inverse
        low = full_dot(cross.T, inverse_ref[leaf, :tile, :tile])
        inverse_ref[leaf, tile:, :tile] = -full_dot(inverse, low)


def corner_factors(where, mine, other, tile, ncols, outer):
    wide = jax.ShapeDtypeStruct((2, 2 * tile, 2 * tile), f32)
    tail = mine.shape[2] - ncols * tile
    hbm = pl.BlockSpec(memory_space=pl.ANY)
    vmem = pl.BlockSpec(memory_space=pltpu.VMEM)
    return pl.pallas_call(
        functools.partial(corner_kernel, (tile, ncols, outer, mine.shape[0])),
        out_shape=[wide, wide],
        in_specs=[pl.BlockSpec(memory_space=pltpu.SMEM), hbm, hbm],
        out_specs=[vmem, vmem],
        scratch_shapes=[
            pltpu.VMEM((2, tile, 2 * tile), f32),
            pltpu.VMEM((2, 2, 2 * tile, tile), bf16),
            pltpu.VMEM((2, 2, tail, tile), bf16),
            pltpu.SemaphoreType.DMA((2, 2)),
        ],
        cost_estimate=pl.CostEstimate(flops=0, bytes_accessed=60_000_000, transcendentals=0),
        name="corner_factors",
    )(where, mine, other)


def split3(x):
    high = x.astype(bf16)
    rest = x - high.astype(f32)
    mid = rest.astype(bf16)
    low = (rest - mid.astype(f32)).astype(bf16)
    return high, mid, low


def solve_kernel(dims, source_ref, where_ref, inverse_ref, upper_ref, mine_ref, other_ref, *rest):
    tile, nrows, ncols, rows, cols, width = dims
    factor_ref, left_ref, right_ref, gains_ref, panel, sem = rest
    row_at = where_ref[1]
    col_at = where_ref[2]
    outer = ncols // rows
    copies = [
        pltpu.make_async_copy(ref.at[k], panel.at[place, lax.rem(col_at + k, cols)], sem)
        for ref, place in ((mine_ref, row_at), (other_ref, 1 - row_at))
        for k in range(cols)
    ]
    for copy in copies:
        copy.start()
    for copy in copies:
        copy.wait()
    for s in range(rows):
        for c in range(cols):
            for leaf in range(2):
                pieces = panel[s, c, leaf, ncols * tile :, :].astype(f32)
                gains_ref[(s * cols + c) * 2 + leaf] = (
                    pieces[:outer] + pieces[outer : 2 * outer] + pieces[2 * outer : 3 * outer]
                )
    col_at = where_ref[2]
    half = nrows * rows // 2
    side = where_ref[0]

    def raw(leaf, block):
        at = block // rows % cols
        j = block // (rows * cols) * rows + block % rows
        lines = pl.ds(pl.multiple_of(j * tile, tile), tile)
        return jnp.concatenate([panel[s, at, leaf, lines, :] for s in range(rows)], axis=0)

    def dots(pieces, value):
        total = jnp.dot(pieces[0], value, preferred_element_type=f32)
        for piece in pieces[1:]:
            total = total + jnp.dot(piece, value, preferred_element_type=f32)
        return total

    own = split3(inverse_ref[0, pl.ds(pl.multiple_of(col_at * width, width), width), :])

    def factor(i, carry):
        factor_ref[i] = dots(own, raw(0, i * rows + row_at))
        return carry

    lax.fori_loop(1, nrows, factor, 0)
    top = upper_ref[0, pl.ds(pl.multiple_of(col_at * width, width), width), :]
    factor_ref[0] = jnp.where(row_at == 0, top[:, :tile], top[:, tile:])
    for leaf in range(2):
        pieces = split3(inverse_ref[leaf])

        def solved(block):
            value = dots(pieces, raw(leaf, jnp.maximum(block, 0)))
            return jnp.where(block >= 0, value, 0.0)

        for j in range(ncols):
            parent = ((j // rows) * cols + col_at) * rows + j % rows
            value = solved(source_ref[leaf, parent])
            high = value.astype(bf16)
            low = (value - high.astype(f32)).astype(bf16)
            depth = rows * tile
            lanes = pl.ds(j * tile, tile)
            right_ref[leaf, :depth, lanes] = high
            right_ref[leaf, depth : 2 * depth, lanes] = low
            right_ref[leaf, 2 * depth :, lanes] = high

        def left(i, carry):
            parent = side * half + i * rows + row_at
            value = solved(source_ref[leaf, parent]).T
            high = value.astype(bf16)
            low = (value - high.astype(f32)).astype(bf16)
            left_ref[leaf, i] = jnp.concatenate([high, high, low], axis=1)
            return carry

        lax.fori_loop(0, nrows // 2, left, 0)


def solved_panels(source, where, inverse, upper, mine, other, dims):
    tile, nrows, ncols, rows, cols, width = dims
    smem = pl.BlockSpec(memory_space=pltpu.SMEM)
    vmem = pl.BlockSpec(memory_space=pltpu.VMEM)
    hbm = pl.BlockSpec(memory_space=pl.ANY)
    depth = 3 * rows * tile
    return pl.pallas_call(
        functools.partial(solve_kernel, dims),
        out_shape=[
            jax.ShapeDtypeStruct((nrows, width, tile), f32),
            jax.ShapeDtypeStruct((2, nrows // 2, tile, depth), bf16),
            jax.ShapeDtypeStruct((2, depth, ncols * tile), bf16),
            jax.ShapeDtypeStruct((rows * cols * 2, ncols // rows, tile), f32),
        ],
        in_specs=[smem, smem, vmem, vmem, hbm, hbm],
        out_specs=[vmem] * 4,
        scratch_shapes=[
            pltpu.VMEM((rows,) + mine.shape, bf16),
            pltpu.SemaphoreType.DMA,
        ],
        compiler_params=pltpu.CompilerParams(vmem_limit_bytes=VMEM_LIMIT),
        cost_estimate=pl.CostEstimate(flops=0, bytes_accessed=1_000_000, transcendentals=0),
        name="solve_panels",
    )(source, where, inverse, upper, mine, other)


def merge_kernel(dims, leaves, source_ref, where_ref, *rest):
    tile, nrows, ncols, rows, cols, group = dims
    count = len(leaves)
    bufs = rest[:count]
    reg_ref, left_ref, right_ref, out_ref = rest[count : count + 4]
    table, blocks, lists_low, lists_v, lists, sem = rest[count + 4 :]
    step = pl.program_id(0)
    side = where_ref[0]
    row_at = where_ref[1]
    col_at = where_ref[2]
    half = nrows * rows // 2
    per_leaf = nrows // 2 * ncols

    @pl.when(step == 0)
    def _():
        def clear(i, carry):
            table[i] = 0
            return carry

        copies = [
            pltpu.make_async_copy(
                bufs[k].at[bufs[k].shape[0] - 1, pl.ds(0, 16)], lists_low.at[k], sem
            )
            for k in range(count)
        ]
        for copy in copies:
            copy.start()
        lax.fori_loop(0, 2 * per_leaf, clear, 0, unroll=16)
        blocks[0] = jnp.zeros((tile, tile), bf16)
        for copy in copies:
            copy.wait()
        for k in range(count):
            listed = lists_low[k].astype(f32)
            codes = listed[0:1] * 256.0 + listed[1:2]
            lists_v[k] = jnp.concatenate([codes, listed[2:4]] + [codes] * 5, axis=0).astype(i32)
        copy = pltpu.make_async_copy(lists_v, lists, sem)
        copy.start()
        copy.wait()
        base = 1
        started = 0
        for k in range(count):
            room = bufs[k].shape[0] - 1
            mine = lists[k, 1 + row_at, 0]
            first = jnp.where(row_at == 0, 0, room - mine)
            parts = lax.div(mine + (PART - 1), PART)

            def fetch(c, carry):
                at = jnp.where(row_at == 0, c * PART, room - PART - c * PART)
                pltpu.make_async_copy(
                    bufs[k].at[pl.ds(at, PART)], blocks.at[pl.ds(base + at, PART)], sem
                ).start()
                return carry

            lax.fori_loop(0, parts, fetch, 0)

            def place(e, carry):
                table[leaves[k] * per_leaf + lists[k, 0, e]] = base + e
                return carry

            lax.fori_loop(first, first + mine, place, 0)
            base = base + room
            started = started + parts

        def drain(_, carry):
            pltpu.make_async_copy(
                bufs[0].at[pl.ds(0, PART)], blocks.at[pl.ds(1, PART)], sem
            ).wait()
            return carry

        lax.fori_loop(0, started, drain, 0)

    def less(slot, update):
        return (blocks[slot].astype(f32) - update).astype(bf16).astype(f32)

    wide = min(2, ncols)
    lefts = [left_ref[leaf].reshape(group * tile, left_ref.shape[-1]) for leaf in range(2)]
    for first in range(0, ncols, wide):
        updates = [
            jnp.dot(
                lefts[leaf],
                right_ref[leaf, :, first * tile : (first + wide) * tile],
                preferred_element_type=f32,
            )
            for leaf in range(2)
        ]
        for g in range(group):
            for w in range(wide):
                j = first + w
                parts = []
                for leaf in range(2):
                    slot = table[leaf * per_leaf + (step * group + g) * ncols + j]
                    update = updates[leaf][g * tile : (g + 1) * tile, w * tile : (w + 1) * tile]
                    parts.append(less(slot, update))
                out_ref[pl.ds(g * tile * ncols + j, tile, stride=ncols), :] = parts[0] + parts[1]

    on_diagonal = lax.broadcasted_iota(i32, (tile, tile), 0) == lax.broadcasted_iota(
        i32, (tile, tile), 1
    )
    for g in range(group):
        place_row = step * group + g
        parent = side * half + place_row * rows + row_at

        @pl.when(parent // rows % cols == col_at)
        def _():
            j = parent // (rows * cols) * rows + parent % rows
            parts = []
            for leaf in range(2):
                block = source_ref[leaf, parent]
                present = jnp.maximum(block, 0)
                at = (present % rows * cols + present // rows % cols) * 2 + leaf
                gain = reg_ref[at, pl.ds(present // (rows * cols), 1), :]
                gain = jnp.where(on_diagonal & (block >= 0), gain, 0.0)
                update = jnp.dot(
                    left_ref[leaf, g],
                    right_ref[leaf, :, pl.ds(pl.multiple_of(j * tile, tile), tile)],
                    preferred_element_type=f32,
                )
                parts.append(less(table[leaf * per_leaf + place_row * ncols + j], update - gain))
            out_ref[pl.ds(g * tile * ncols + j, tile, stride=ncols), :] = parts[0] + parts[1]


def merged_parent(source, where, bufs, leaves, reg, left, right, dims):
    tile, nrows, ncols, rows, cols, group = dims
    count = len(leaves)
    smem = pl.BlockSpec(memory_space=pltpu.SMEM)
    hbm = pl.BlockSpec(memory_space=pl.ANY)
    vmem = pl.BlockSpec(memory_space=pltpu.VMEM)
    depth = left.shape[-1]
    return pl.pallas_call(
        functools.partial(merge_kernel, dims, leaves),
        out_shape=jax.ShapeDtypeStruct((nrows // 2 * tile * ncols, tile), f32),
        grid=(nrows // 2 // group,),
        in_specs=[smem] * 2
        + [hbm] * count
        + [
            vmem,
            pl.BlockSpec((2, group, tile, depth), lambda i: (0, i, 0, 0)),
            vmem,
        ],
        out_specs=pl.BlockSpec((group * tile * ncols, tile), lambda i: (i, 0)),
        scratch_shapes=[
            pltpu.SMEM((nrows * ncols,), i32),
            pltpu.VMEM((1 + sum(buf.shape[0] - 1 for buf in bufs), tile, tile), bf16),
            pltpu.VMEM((count, 16, tile), bf16),
            pltpu.VMEM((count, 8, tile), i32),
            pltpu.SMEM((count, 8, tile), i32),
            pltpu.SemaphoreType.DMA,
        ],
        compiler_params=pltpu.CompilerParams(vmem_limit_bytes=VMEM_LIMIT),
        name="merge_parent",
    )(source, where, *bufs, reg, left, right)


def sparse_sources(child_map, blocks, panel_blocks):
    targets = child_map[:, None, :]
    matches = targets == jnp.arange(blocks, dtype=i32)[None, :, None]
    ids = panel_blocks + jnp.arange(child_map.shape[1], dtype=i32)
    return jnp.sum(jnp.where(matches, ids + 1, 0), axis=2) - 1


def shards(front_tiles, regular, child_map):
    rows = lax.axis_size("row")
    cols = lax.axis_size("col")
    leaves = lax.axis_size("leaf")
    row_at = lax.axis_index("row")
    col_at = lax.axis_index("col")
    side = lax.axis_index("leaf") % 2
    tile = front_tiles.shape[-1]
    outer = front_tiles.shape[1]
    nrows = outer * cols
    ncols = outer * rows
    blocks = nrows * rows
    cap = -(-nrows * ncols * 5 // 256) * 8
    spill = -(-cap // (5 * PART)) * PART
    rooms = (cap,) * 2 + (cap - spill,) * 3 + (spill,) * 3
    width = NPAN * rows * tile // cols
    group = 2
    where = jnp.stack([side, row_at, col_at]).astype(i32)
    flat = front_tiles.reshape(nrows * tile * ncols, tile)
    leaf_pairs = [(i, i ^ 1) for i in range(leaves)]
    col_pairs = [(i, (i - 1) % cols) for i in range(cols)]
    row_pairs = [(i, (i + 1) % rows) for i in range(rows)]
    both_pairs = [
        (i * cols + j, (i ^ 1) * cols + (j - 1) % cols)
        for i in range(leaves)
        for j in range(cols)
    ]

    def from_each_col(value):
        pairs = [[(j, (j - k) % cols) for j in range(cols)] for k in range(cols)]
        return [value] + [lax.ppermute(value, "col", pairs[k]) for k in range(1, cols)]

    own_panel = panel_and_gains(flat, regular.reshape(outer, tile), tile, ncols)
    own_map = child_map.reshape(-1)
    sib_panel = lax.ppermute(own_panel, "leaf", leaf_pairs)
    sib_map = lax.ppermute(own_map, "leaf", leaf_pairs)
    own_panels = from_each_col(own_panel)
    hits = block_flags(flat, tile, nrows, ncols)
    moves = block_moves(own_map, side, row_at, col_at, nrows, ncols, rows, cols)
    entries = jnp.where(hits[0] > 0, moves, -1)
    kinds = jnp.arange(5, dtype=i32)[:, None]
    counts = jnp.sum(((entries >= 0)[None, :] & (entries % 8 == kinds)).astype(i32), axis=1)
    first_room = cap - spill
    stats = jnp.stack(
        [
            jnp.max(counts) > cap,
            jnp.maximum(counts[2], counts[4]) > first_room,
            counts[3] > first_room,
        ]
    ).astype(i32)
    sib_panel, sib_map, entries, stats = lax.optimization_barrier(
        (sib_panel, sib_map, entries, stats)
    )
    stats = jnp.maximum(stats, lax.ppermute(stats, "leaf", leaf_pairs))
    mark_row = own_panel.shape[0] - 1
    mark = jnp.pad(stats.astype(bf16), (0, tile - 3))[None, :]
    sib_panel = lax.dynamic_update_slice(sib_panel, mark, (mark_row, 0))
    sib_panels = from_each_col(sib_panel)
    maps = jnp.stack([own_map, sib_map])
    source = sparse_sources(maps, blocks, NPAN * rows)
    found = sorted_blocks(flat, entries, (tile, nrows, ncols, rows, rooms))
    found, own_panels, sib_panels, source = lax.optimization_barrier(
        (found, own_panels, sib_panels, source)
    )
    kept, row_move, col_move, leaf_move, far_move, col_more, leaf_more, far_more = found
    far = lax.ppermute(far_move, ("leaf", "col"), both_pairs)
    beside = lax.ppermute(leaf_move, "leaf", leaf_pairs)
    near = lax.ppermute(col_move, "col", col_pairs)
    across = lax.ppermute(row_move, "row", row_pairs)
    mine = jnp.stack([jnp.stack(pair) for pair in zip(own_panels, sib_panels)])
    other = lax.ppermute(mine, "row", row_pairs)
    inverse, upper = corner_factors(where, mine, other, tile, ncols, outer)
    factor, left, right, reg = solved_panels(
        source, where, inverse, upper, mine, other, (tile, nrows, ncols, rows, cols, width)
    )
    marks = jnp.concatenate([mine[:, 1, mark_row, :3], other[:, 1, mark_row, :3]])
    marks = jnp.max(marks.astype(f32), axis=0) > 0
    near, beside, far, left, right, marks = lax.optimization_barrier(
        (near, beside, far, left, right, marks)
    )
    over = marks[0]

    def rest_of(cols_too, leaves_too):
        def branch(near, beside, far, col_more, leaf_more, far_more):
            if cols_too:
                far_more = lax.ppermute(far_more, ("leaf", "col"), both_pairs)
                col_more = lax.ppermute(col_more, "col", col_pairs)
            if leaves_too:
                leaf_more = lax.ppermute(leaf_more, "leaf", leaf_pairs)
            firsts = [lax.ppermute(v, "row", row_pairs) for v in (near, beside, far)]
            more = [col_more, leaf_more, far_more]
            crossed = [
                lax.ppermute(v, "row", row_pairs) if sent else v
                for v, sent in zip(more, (cols_too, leaves_too, cols_too))
            ]
            return firsts, more, crossed

        return branch

    firsts, more, crossed = lax.switch(
        marks[1].astype(i32) * 2 + marks[2].astype(i32),
        [rest_of(i // 2 == 1, i % 2 == 1) for i in range(4)],
        near, beside, far, col_more, leaf_more, far_more,
    )
    bufs = [kept, across, near, beside, far] + firsts + more + crossed
    owners = (0, 0) + (0, 1, 1) * 4

    def sparse():
        return merged_parent(
            source, where, bufs, owners, reg, left, right,
            (tile, nrows, ncols, rows, cols, group),
        )

    def dense():
        own = untangled(flat, tile, ncols)
        other = lax.ppermute(own, "row", row_pairs)
        places = jnp.arange(ncols, dtype=i32)
        col_source = source[0][((places // rows) * cols + col_at) * rows + places % rows]
        col_index = jnp.maximum(col_source, 0)
        col_index = col_index // (rows * cols) * rows + col_index % rows
        from_next = (col_source // rows % cols != col_at)[None, :, None, None]
        col_present = (col_source >= 0)[None, :, None, None]
        halves = []
        for half in range(2):
            half_rows = half * (nrows // 2) + jnp.arange(nrows // 2, dtype=i32)
            row_source = source[0][half_rows * rows + row_at]
            row_index = jnp.maximum(row_source, 0) // rows
            is_own = (row_source % rows == row_at)[:, None, None, None]
            picked = jnp.where(
                is_own, jnp.take(own, row_index, axis=0), jnp.take(other, row_index, axis=0)
            )
            picked = jnp.where((row_source >= 0)[:, None, None, None], picked, jnp.zeros_like(picked))
            following = lax.ppermute(picked, "col", col_pairs)
            picked = jnp.where(
                from_next,
                jnp.take(following, col_index, axis=1),
                jnp.take(picked, col_index, axis=1),
            )
            picked = jnp.where(col_present, picked, jnp.zeros_like(picked))
            halves.append(picked.reshape(nrows * ncols // 2, tile, tile))
        stays = jnp.where(side == 0, halves[0], halves[1])
        leaves_here = jnp.where(side == 0, halves[1], halves[0])
        arrived = lax.ppermute(leaves_here, "leaf", leaf_pairs)
        every = nrows * ncols // 2
        part = min(every, tile)
        bufs = []
        for value in (stays, arrived):
            for first in range(0, every, part):
                codes = first + jnp.arange(tile, dtype=i32)
                full = jnp.full((tile,), part, i32)
                listed = jnp.stack([codes // 256, codes % 256, full, full])
                listed = jnp.pad(listed, ((0, tile - 4), (0, 0))).astype(bf16)
                bufs.append(jnp.concatenate([value[first : first + part], listed[None]]))
        owners = (0,) * (len(bufs) // 2) + (1,) * (len(bufs) // 2)
        return merged_parent(
            source, where, bufs, owners, reg, left, right,
            (tile, nrows, ncols, rows, cols, group),
        )

    merged = lax.cond(over, dense, sparse)
    factor = factor.reshape(1, outer, cols, 1, width, tile).swapaxes(4, 5)
    merged = merged.reshape(1, outer // 2, cols, 1, tile, outer, 1, rows, tile)
    return factor, merged


def solution(mesh):
    return jax.shard_map(
        shards,
        mesh=mesh,
        in_specs=(
            P("leaf", None, None, "row", None, None, "col", None, None),
            P("leaf", None, "col", "row", None),
            P("leaf", None),
        ),
        out_specs=(
            P("leaf", None, None, "row", None, "col"),
            P("leaf", None, None, "row", None, None, "col", None, None),
        ),
        check_vma=False,
    )
```

```python
import functools

import jax
import jax.numpy as jnp
from jax import lax
from jax.experimental import pallas as pl
from jax.experimental.pallas import tpu as pltpu
from jax.sharding import PartitionSpec as P

NPAN = 1
VMEM_LIMIT = 60 * 1024 * 1024
PART = 8
f32 = jnp.float32
bf16 = jnp.bfloat16
i32 = jnp.int32
HIGHEST = lax.Precision.HIGHEST


def untangle_kernel(tile, ncols, x_ref, out_ref, wide):
    wide[...] = x_ref[...].astype(f32)
    for j in range(ncols):
        out_ref[j] = wide[pl.ds(j, tile, stride=ncols), :].astype(bf16)


def untangled(x, tile, ncols, start, count):
    return pl.pallas_call(
        functools.partial(untangle_kernel, tile, ncols),
        out_shape=jax.ShapeDtypeStruct((count, ncols, tile, tile), bf16),
        scratch_shapes=[pltpu.VMEM((tile * ncols, tile), f32)],
        grid=(count,),
        in_specs=[pl.BlockSpec((tile * ncols, tile), lambda i: (i + start, 0))],
        out_specs=pl.BlockSpec((None, ncols, tile, tile), lambda i: (i, 0, 0, 0)),
        name="untangle",
    )(x)


def panel_kernel(tile, ncols, outer, x_ref, reg_ref, out_ref, wide):
    wide[...] = x_ref[...].astype(f32)
    for j in range(ncols):
        out_ref[pl.ds(j * tile, tile)] = wide[pl.ds(j, tile, stride=ncols), :].astype(bf16)
    pieces = [piece.astype(f32) for piece in split3(reg_ref[...])]
    pad = out_ref.shape[0] - ncols * tile - 3 * outer
    tail = jnp.concatenate(pieces + [jnp.zeros((pad, tile), f32)], axis=0)
    out_ref[pl.ds(ncols * tile, 3 * outer + pad)] = tail.astype(bf16)


def panel_and_gains(x, reg, tile, ncols):
    outer = reg.shape[0]
    tail = -(-(3 * outer + 1) // 16) * 16
    return pl.pallas_call(
        functools.partial(panel_kernel, tile, ncols, outer),
        out_shape=jax.ShapeDtypeStruct((ncols * tile + tail, tile), bf16),
        scratch_shapes=[pltpu.VMEM((tile * ncols, tile), f32)],
        grid=(1,),
        in_specs=[
            pl.BlockSpec((tile * ncols, tile), lambda i: (0, 0)),
            pl.BlockSpec((outer, tile), lambda i: (0, 0)),
        ],
        out_specs=pl.BlockSpec((ncols * tile + tail, tile), lambda i: (0, 0)),
        name="panel_and_gains",
    )(x, reg)


def flag_kernel(tile, ncols, move_ref, x_ref, entry_ref, count_ref, seen):
    step = pl.program_id(0)
    lines = tile * ncols
    group = x_ref.shape[0] // lines
    for g in range(group):
        x = x_ref[g * lines : (g + 1) * lines]
        at = pl.multiple_of((step * group + g) * ncols, ncols)
        if ncols % 16 == 0:
            top = jnp.max(jnp.abs(x).reshape(tile, ncols, tile), axis=0)
            seen[pl.ds(at, ncols)] = top.astype(f32)
        else:
            top = jnp.max(jnp.abs(x.astype(f32)).reshape(tile, ncols, tile), axis=0)
            for j in range(ncols):
                seen[pl.ds(at + j, 1)] = top[j : j + 1]

    @pl.when(step == pl.num_programs(0) - 1)
    def _():
        along = (((1,), (1,)), ((), ()))
        hits = lax.dot_general(
            jnp.ones((8, tile), f32),
            jnp.where(seen[...] > 0, 1.0, 0.0),
            along,
            preferred_element_type=f32,
        )
        moves = jnp.broadcast_to(move_ref[...], hits.shape)
        entries = jnp.where(hits > 0, moves, -1)
        entry_ref[...] = entries
        kinds = jnp.where(entries[:1] >= 0, entries[:1] & 7, -1)
        ids = lax.broadcasted_iota(i32, (tile, hits.shape[1]), 0)
        count_ref[...] = lax.dot_general(
            jnp.ones(hits.shape, f32),
            jnp.where(ids == kinds, 1.0, 0.0),
            along,
            preferred_element_type=f32,
        )


def block_entries(x, moves, tile, nrows, ncols):
    count = nrows * ncols
    return pl.pallas_call(
        functools.partial(flag_kernel, tile, ncols),
        out_shape=[
            jax.ShapeDtypeStruct((8, count), i32),
            jax.ShapeDtypeStruct((8, tile), f32),
        ],
        grid=(nrows // 8,),
        in_specs=[
            pl.BlockSpec((1, count), lambda i: (0, 0)),
            pl.BlockSpec((8 * tile * ncols, tile), lambda i: (i, 0)),
        ],
        out_specs=[
            pl.BlockSpec((8, count), lambda i: (0, 0)),
            pl.BlockSpec((8, tile), lambda i: (0, 0)),
        ],
        scratch_shapes=[pltpu.VMEM((count, tile), f32)],
        compiler_params=pltpu.CompilerParams(vmem_limit_bytes=VMEM_LIMIT),
        cost_estimate=pl.CostEstimate(flops=0, bytes_accessed=30_000_000, transcendentals=0),
        name="block_entries",
    )(moves, x)


def sort_kernel(dims, entry_ref, x_ref, *rest):
    tile, group, ncols, rows, rooms = dims
    regions = len(rooms)
    bufs = rest[:regions]
    wide, blocks, lists, lists_low, counts, sem = rest[regions:]
    step = pl.program_id(0)
    lines = tile * ncols
    lane = lax.broadcasted_iota(i32, (8, tile), 1)
    sublane = lax.broadcasted_iota(i32, (8, tile), 0)

    @pl.when(step == 0)
    def _():
        lists[...] = jnp.zeros_like(lists)
        for k in range(regions * 2):
            counts[k] = 0

    for g in range(group):
        wide[g] = x_ref[g * lines : (g + 1) * lines].astype(f32)

    def one_row(g, carry):
        for j in range(ncols):
            at = (step * group + g) * ncols + j
            entry = entry_ref[0, at]

            @pl.when(entry >= 0)
            def _():
                kind = entry % 8
                end = entry // 8 % rows
                code = entry // (8 * rows)
                held = counts[kind * 2] + counts[kind * 2 + 1]
                spills = (kind >= 2) & (held >= rooms[2])
                region = jnp.where(spills, kind + 3, kind)
                room = jnp.where(spills, rooms[5], jnp.where(kind >= 2, rooms[2], rooms[0]))
                front = counts[region * 2]
                back = counts[region * 2 + 1]
                slot = jnp.where(end == 0, front, room - 1 - back)

                @pl.when(front + back < room)
                def _():
                    counts[region * 2 + end] = jnp.where(end == 0, front, back) + 1
                    blocks[at] = wide[g, pl.ds(j, tile, stride=ncols), :].astype(bf16)
                    here = jnp.where(sublane == 0, code // 256, code % 256).astype(f32)
                    lists[region] = jnp.where(lane == slot, here, lists[region])
                    for k in range(regions):

                        @pl.when(region == k)
                        def _():
                            pltpu.make_async_copy(blocks.at[at], bufs[k].at[slot], sem).start()

        return carry

    lax.fori_loop(0, group, one_row, 0)

    @pl.when(step == pl.num_programs(0) - 1)
    def _():
        sent = 0
        for k in range(regions):
            front = counts[2 * k]
            back = counts[2 * k + 1]
            sent = sent + front + back
            listed = jnp.where(sublane == 2, front.astype(f32), lists[k])
            listed = jnp.where(sublane == 3, back.astype(f32), listed)
            lists_low[k] = jnp.concatenate([listed, listed], axis=0).astype(bf16)
        copies = [
            pltpu.make_async_copy(lists_low.at[k], bufs[k].at[rooms[k], pl.ds(0, 16)], sem)
            for k in range(regions)
        ]
        for copy in copies:
            copy.start()

        def drain(_, carry):
            pltpu.make_async_copy(blocks.at[0], bufs[0].at[0], sem).wait()
            return carry

        lax.fori_loop(0, sent, drain, 0)
        for copy in copies:
            copy.wait()


def sorted_blocks(x, entries, dims):
    tile, nrows, ncols, rows, rooms = dims
    group = 4
    return pl.pallas_call(
        functools.partial(sort_kernel, (tile, group, ncols, rows, rooms)),
        out_shape=[jax.ShapeDtypeStruct((room + 1, tile, tile), bf16) for room in rooms],
        grid=(nrows // group,),
        in_specs=[
            pl.BlockSpec(memory_space=pltpu.SMEM),
            pl.BlockSpec((group * tile * ncols, tile), lambda i: (i, 0)),
        ],
        out_specs=[pl.BlockSpec(memory_space=pl.ANY)] * len(rooms),
        scratch_shapes=[
            pltpu.VMEM((group, tile * ncols, tile), f32),
            pltpu.VMEM((nrows * ncols, tile, tile), bf16),
            pltpu.VMEM((len(rooms), 8, tile), f32),
            pltpu.VMEM((len(rooms), 16, tile), bf16),
            pltpu.SMEM((len(rooms) * 2,), i32),
            pltpu.SemaphoreType.DMA,
        ],
        compiler_params=pltpu.CompilerParams(vmem_limit_bytes=VMEM_LIMIT),
        cost_estimate=pl.CostEstimate(flops=0, bytes_accessed=60_000_000, transcendentals=0),
        name="sort_blocks",
    )(entries, x)


def block_moves(own_map, side, row_at, col_at, nrows, ncols, rows, cols):
    parent = jnp.concatenate([jnp.full((NPAN * rows,), -1, i32), own_map])
    at_row = parent.reshape(nrows, rows)
    at_row = jnp.where(row_at == 0, at_row[:, 0], at_row[:, 1])[:, None]
    at_col = parent.reshape(nrows // cols, cols, rows)
    at_col = lax.dynamic_index_in_dim(at_col, col_at, 1, keepdims=False).reshape(1, ncols)
    moves_leaf = at_row // (nrows * rows // 2) != side
    moves_col = at_col // rows % cols != col_at
    moves_row = at_row % rows != row_at
    kind = jnp.where(
        moves_leaf,
        jnp.where(moves_col, 4, 3),
        jnp.where(moves_col, 2, jnp.where(moves_row, 1, 0)),
    )
    place_row = at_row // rows % (nrows // 2)
    place_col = at_col // (rows * cols) * rows + at_col % rows
    code = (place_row * ncols + place_col) * rows + at_row % rows
    return jnp.where((at_row >= 0) & (at_col >= 0), code * 8 + kind, -1).reshape(-1)


def eliminate(works, tile):
    rows = lax.broadcasted_iota(i32, (tile, tile), 0)
    lanes = lax.broadcasted_iota(i32, (tile, tile), 1)
    lane_row = lax.broadcasted_iota(i32, (1, tile), 1)

    def one(k, carry):
        values = [work[...] for work in works]
        pivot_rows = [work[pl.ds(k, 1), :] for work in works]
        done = []
        for value, pivot_row in zip(values, pivot_rows):
            column = jnp.sum(jnp.where(lanes == k, value[:, :tile], 0.0), axis=1, keepdims=True)
            pivot = jnp.sum(
                jnp.where(lane_row == k, pivot_row[:, :tile], 0.0), axis=1, keepdims=True
            )
            ratio = jnp.where(rows[:, :1] > k, column, 0.0)
            done.append(value - ratio * (pivot_row * (1.0 / pivot)))
        for work, value in zip(works, done):
            work[...] = value
        return carry

    lax.fori_loop(0, tile, one, 0)


def full_dot(a, b):
    return jnp.dot(a, b, precision=HIGHEST, preferred_element_type=f32)


def corner_kernel(dims, where_ref, *rest):
    tile, ncols, outer, cols = dims
    panels = [rest[kind * cols : (kind + 1) * cols] for kind in range(4)]
    inverse_ref, upper_ref, first_work, second_work, tiles, tails, sem = rest[4 * cols :]
    works = (first_work, second_work)
    row_at = where_ref[1]
    first = lax.rem(cols - where_ref[2], cols)
    tail = tails.shape[2]
    for kind in range(4):
        at = row_at if kind < 2 else 1 - row_at
        leaf = kind % 2

        def copies(ref):
            return (
                pltpu.make_async_copy(ref.at[pl.ds(0, 2 * tile)], tiles.at[at, leaf], sem.at[0, kind]),
                pltpu.make_async_copy(
                    ref.at[pl.ds(ncols * tile, tail)], tails.at[at, leaf], sem.at[1, kind]
                ),
            )

        for k in range(cols):

            @pl.when(first == k)
            def _():
                for copy in copies(panels[kind][k]):
                    copy.start()

    for kind in range(4):
        at = row_at if kind < 2 else 1 - row_at
        pltpu.make_async_copy(
            panels[kind][0].at[pl.ds(0, 2 * tile)], tiles.at[at, kind % 2], sem.at[0, kind]
        ).wait()
        pltpu.make_async_copy(
            panels[kind][0].at[pl.ds(ncols * tile, tail)], tails.at[at, kind % 2], sem.at[1, kind]
        ).wait()
    rows = lax.broadcasted_iota(i32, (tile, tile), 0)
    lanes = lax.broadcasted_iota(i32, (tile, tile), 1)
    eye = jnp.where(rows == lanes, 1.0, 0.0).astype(f32)

    def block(leaf, i, j):
        value = tiles[i, leaf, j * tile : (j + 1) * tile, :].astype(f32)
        if i == j:
            pieces = tails[i, leaf].astype(f32)
            gain = pieces[:1] + pieces[outer : outer + 1] + pieces[2 * outer : 2 * outer + 1]
            value = value + jnp.where(rows == lanes, gain, 0.0)
        return value

    def finish(leaf):
        upper = works[leaf][:, :tile]
        unit = works[leaf][:, tile:]
        pivots = jnp.sum(jnp.where(rows == lanes, upper, 0.0), axis=1, keepdims=True)
        scale = 1.0 / jnp.sqrt(pivots)
        return jnp.where(lanes >= rows, upper * scale, 0.0), jnp.where(
            lanes <= rows, unit * scale, 0.0
        )

    for leaf in range(2):
        works[leaf][:, :tile] = block(leaf, 0, 0)
        works[leaf][:, tile:] = eye
    eliminate(works, tile)
    for leaf in range(2):
        upper, inverse = finish(leaf)
        cross = full_dot(inverse, block(leaf, 0, 1))
        upper_ref[leaf, :tile, :tile] = upper
        upper_ref[leaf, :tile, tile:] = cross
        upper_ref[leaf, tile:, :tile] = jnp.zeros((tile, tile), f32)
        inverse_ref[leaf, :tile, :tile] = inverse
        inverse_ref[leaf, :tile, tile:] = jnp.zeros((tile, tile), f32)
        works[leaf][:, :tile] = block(leaf, 1, 1) - full_dot(cross.T, cross)
        works[leaf][:, tile:] = eye
    eliminate(works, tile)
    for leaf in range(2):
        upper, inverse = finish(leaf)
        cross = upper_ref[leaf, :tile, tile:]
        upper_ref[leaf, tile:, tile:] = upper
        inverse_ref[leaf, tile:, tile:] = inverse
        low = full_dot(cross.T, inverse_ref[leaf, :tile, :tile])
        inverse_ref[leaf, tile:, :tile] = -full_dot(inverse, low)


def corner_factors(where, panels, tile, ncols, outer):
    wide = jax.ShapeDtypeStruct((2, 2 * tile, 2 * tile), f32)
    cols = len(panels[0])
    tail = panels[0][0].shape[0] - ncols * tile
    hbm = pl.BlockSpec(memory_space=pl.ANY)
    vmem = pl.BlockSpec(memory_space=pltpu.VMEM)
    return pl.pallas_call(
        functools.partial(corner_kernel, (tile, ncols, outer, cols)),
        out_shape=[wide, wide],
        in_specs=[pl.BlockSpec(memory_space=pltpu.SMEM)] + [hbm] * (4 * cols),
        out_specs=[vmem, vmem],
        scratch_shapes=[
            pltpu.VMEM((tile, 2 * tile), f32),
            pltpu.VMEM((tile, 2 * tile), f32),
            pltpu.VMEM((2, 2, 2 * tile, tile), bf16),
            pltpu.VMEM((2, 2, tail, tile), bf16),
            pltpu.SemaphoreType.DMA((2, 4)),
        ],
        cost_estimate=pl.CostEstimate(flops=0, bytes_accessed=60_000_000, transcendentals=0),
        name="corner_factors",
    )(where, *[value for kind in panels for value in kind])


def split3(x):
    high = x.astype(bf16)
    rest = x - high.astype(f32)
    mid = rest.astype(bf16)
    low = (rest - mid.astype(f32)).astype(bf16)
    return high, mid, low


def solve_kernel(dims, source_ref, where_ref, inverse_ref, upper_ref, *rest):
    tile, nrows, ncols, rows, cols, width = dims
    given = rest[: 4 * cols]
    factor_ref, left_ref, right_ref, gains_ref, panel, sem = rest[4 * cols :]
    row_at = where_ref[1]
    col_at = where_ref[2]
    outer = ncols // rows
    copies = [
        pltpu.make_async_copy(
            given[kind * cols + k],
            panel.at[row_at if kind < 2 else 1 - row_at, lax.rem(col_at + k, cols), kind % 2],
            sem,
        )
        for kind in range(4)
        for k in range(cols)
    ]
    for copy in copies:
        copy.start()
    for copy in copies:
        copy.wait()
    for s in range(rows):
        for c in range(cols):
            for leaf in range(2):
                pieces = panel[s, c, leaf, ncols * tile :, :].astype(f32)
                gains_ref[(s * cols + c) * 2 + leaf] = (
                    pieces[:outer] + pieces[outer : 2 * outer] + pieces[2 * outer : 3 * outer]
                )
    col_at = where_ref[2]
    half = nrows * rows // 2
    side = where_ref[0]

    def raw(leaf, block):
        at = block // rows % cols
        j = block // (rows * cols) * rows + block % rows
        lines = pl.ds(pl.multiple_of(j * tile, tile), tile)
        return jnp.concatenate([panel[s, at, leaf, lines, :] for s in range(rows)], axis=0)

    def dots(pieces, value):
        total = jnp.dot(pieces[0], value, preferred_element_type=f32)
        for piece in pieces[1:]:
            total = total + jnp.dot(piece, value, preferred_element_type=f32)
        return total

    own = split3(inverse_ref[0, pl.ds(pl.multiple_of(col_at * width, width), width), :])

    def factor(i, carry):
        factor_ref[i] = dots(own, raw(0, i * rows + row_at))
        return carry

    lax.fori_loop(1, nrows, factor, 0, unroll=4)
    top = upper_ref[0, pl.ds(pl.multiple_of(col_at * width, width), width), :]
    factor_ref[0] = jnp.where(row_at == 0, top[:, :tile], top[:, tile:])
    for leaf in range(2):
        pieces = split3(inverse_ref[leaf])

        def solved(block):
            value = dots(pieces, raw(leaf, jnp.maximum(block, 0)))
            return jnp.where(block >= 0, value, 0.0)

        for j in range(ncols):
            parent = ((j // rows) * cols + col_at) * rows + j % rows
            value = solved(source_ref[leaf, parent])
            high = value.astype(bf16)
            low = (value - high.astype(f32)).astype(bf16)
            depth = rows * tile
            lanes = pl.ds(j * tile, tile)
            right_ref[leaf, :depth, lanes] = high
            right_ref[leaf, depth : 2 * depth, lanes] = low
            right_ref[leaf, 2 * depth :, lanes] = high

        def left(i, carry):
            parent = side * half + i * rows + row_at
            value = solved(source_ref[leaf, parent]).T
            high = value.astype(bf16)
            low = (value - high.astype(f32)).astype(bf16)
            left_ref[leaf, i] = jnp.concatenate([high, high, low], axis=1)
            return carry

        lax.fori_loop(0, nrows // 2, left, 0, unroll=4)


def solved_panels(source, where, inverse, upper, panels, dims):
    tile, nrows, ncols, rows, cols, width = dims
    smem = pl.BlockSpec(memory_space=pltpu.SMEM)
    vmem = pl.BlockSpec(memory_space=pltpu.VMEM)
    hbm = pl.BlockSpec(memory_space=pl.ANY)
    depth = 3 * rows * tile
    return pl.pallas_call(
        functools.partial(solve_kernel, dims),
        out_shape=[
            jax.ShapeDtypeStruct((nrows, width, tile), f32),
            jax.ShapeDtypeStruct((2, nrows // 2, tile, depth), bf16),
            jax.ShapeDtypeStruct((2, depth, ncols * tile), bf16),
            jax.ShapeDtypeStruct((rows * cols * 2, ncols // rows, tile), f32),
        ],
        in_specs=[smem, smem, vmem, vmem] + [hbm] * (4 * cols),
        out_specs=[vmem] * 4,
        scratch_shapes=[
            pltpu.VMEM((rows, cols, 2) + panels[0][0].shape, bf16),
            pltpu.SemaphoreType.DMA,
        ],
        compiler_params=pltpu.CompilerParams(vmem_limit_bytes=VMEM_LIMIT),
        cost_estimate=pl.CostEstimate(flops=0, bytes_accessed=1_000_000, transcendentals=0),
        name="solve_panels",
    )(source, where, inverse, upper, *[value for kind in panels for value in kind])


def merge_kernel(dims, leaves, source_ref, where_ref, *rest):
    tile, nrows, ncols, rows, cols, group = dims
    count = len(leaves)
    bufs = rest[:count]
    reg_ref, left_ref, right_ref, out_ref = rest[count : count + 4]
    table, blocks, lists_low, lists_v, lists, sem = rest[count + 4 :]
    step = pl.program_id(0)
    side = where_ref[0]
    row_at = where_ref[1]
    col_at = where_ref[2]
    half = nrows * rows // 2
    per_leaf = nrows // 2 * ncols

    @pl.when(step == 0)
    def _():
        def clear(i, carry):
            table[i] = 0
            return carry

        copies = [
            pltpu.make_async_copy(
                bufs[k].at[bufs[k].shape[0] - 1, pl.ds(0, 16)], lists_low.at[k], sem
            )
            for k in range(count)
        ]
        for copy in copies:
            copy.start()
        lax.fori_loop(0, 2 * per_leaf, clear, 0, unroll=16)
        blocks[0] = jnp.zeros((tile, tile), bf16)
        for copy in copies:
            copy.wait()
        for k in range(count):
            listed = lists_low[k].astype(f32)
            codes = listed[0:1] * 256.0 + listed[1:2]
            lists_v[k] = jnp.concatenate([codes, listed[2:4]] + [codes] * 5, axis=0).astype(i32)
        copy = pltpu.make_async_copy(lists_v, lists, sem)
        copy.start()
        copy.wait()
        base = 1
        started = 0
        for k in range(count):
            room = bufs[k].shape[0] - 1
            mine = lists[k, 1 + row_at, 0]
            first = jnp.where(row_at == 0, 0, room - mine)
            parts = lax.div(mine + (PART - 1), PART)

            def fetch(c, carry):
                at = jnp.where(row_at == 0, c * PART, room - PART - c * PART)
                pltpu.make_async_copy(
                    bufs[k].at[pl.ds(at, PART)], blocks.at[pl.ds(base + at, PART)], sem
                ).start()
                return carry

            lax.fori_loop(0, parts, fetch, 0)

            def place(e, carry):
                table[leaves[k] * per_leaf + lists[k, 0, e]] = base + e
                return carry

            lax.fori_loop(first, first + mine, place, 0)
            base = base + room
            started = started + parts

        def drain(_, carry):
            pltpu.make_async_copy(
                bufs[0].at[pl.ds(0, PART)], blocks.at[pl.ds(1, PART)], sem
            ).wait()
            return carry

        lax.fori_loop(0, started, drain, 0)

    def less(slot, update):
        return (blocks[slot].astype(f32) - update).astype(bf16).astype(f32)

    wide = min(2, ncols)
    lefts = [left_ref[leaf].reshape(group * tile, left_ref.shape[-1]) for leaf in range(2)]
    for first in range(0, ncols, wide):
        updates = [
            jnp.dot(
                lefts[leaf],
                right_ref[leaf, :, first * tile : (first + wide) * tile],
                preferred_element_type=f32,
            )
            for leaf in range(2)
        ]
        for g in range(group):
            for w in range(wide):
                j = first + w
                parts = []
                for leaf in range(2):
                    slot = table[leaf * per_leaf + (step * group + g) * ncols + j]
                    update = updates[leaf][g * tile : (g + 1) * tile, w * tile : (w + 1) * tile]
                    parts.append(less(slot, update))
                out_ref[pl.ds(g * tile * ncols + j, tile, stride=ncols), :] = parts[0] + parts[1]

    on_diagonal = lax.broadcasted_iota(i32, (tile, tile), 0) == lax.broadcasted_iota(
        i32, (tile, tile), 1
    )
    for g in range(group):
        place_row = step * group + g
        parent = side * half + place_row * rows + row_at

        @pl.when(parent // rows % cols == col_at)
        def _():
            j = parent // (rows * cols) * rows + parent % rows
            parts = []
            for leaf in range(2):
                block = source_ref[leaf, parent]
                present = jnp.maximum(block, 0)
                at = (present % rows * cols + present // rows % cols) * 2 + leaf
                gain = reg_ref[at, pl.ds(present // (rows * cols), 1), :]
                gain = jnp.where(on_diagonal & (block >= 0), gain, 0.0)
                update = jnp.dot(
                    left_ref[leaf, g],
                    right_ref[leaf, :, pl.ds(pl.multiple_of(j * tile, tile), tile)],
                    preferred_element_type=f32,
                )
                parts.append(less(table[leaf * per_leaf + place_row * ncols + j], update - gain))
            out_ref[pl.ds(g * tile * ncols + j, tile, stride=ncols), :] = parts[0] + parts[1]


def merged_parent(source, where, bufs, leaves, reg, left, right, dims):
    tile, nrows, ncols, rows, cols, group = dims
    count = len(leaves)
    smem = pl.BlockSpec(memory_space=pltpu.SMEM)
    hbm = pl.BlockSpec(memory_space=pl.ANY)
    vmem = pl.BlockSpec(memory_space=pltpu.VMEM)
    depth = left.shape[-1]
    return pl.pallas_call(
        functools.partial(merge_kernel, dims, leaves),
        out_shape=jax.ShapeDtypeStruct((nrows // 2 * tile * ncols, tile), f32),
        grid=(nrows // 2 // group,),
        in_specs=[smem] * 2
        + [hbm] * count
        + [
            vmem,
            pl.BlockSpec((2, group, tile, depth), lambda i: (0, i, 0, 0)),
            vmem,
        ],
        out_specs=pl.BlockSpec((group * tile * ncols, tile), lambda i: (i, 0)),
        scratch_shapes=[
            pltpu.SMEM((nrows * ncols,), i32),
            pltpu.VMEM((1 + sum(buf.shape[0] - 1 for buf in bufs), tile, tile), bf16),
            pltpu.VMEM((count, 16, tile), bf16),
            pltpu.VMEM((count, 8, tile), i32),
            pltpu.SMEM((count, 8, tile), i32),
            pltpu.SemaphoreType.DMA,
        ],
        compiler_params=pltpu.CompilerParams(vmem_limit_bytes=VMEM_LIMIT),
        name="merge_parent",
    )(source, where, *bufs, reg, left, right)


def sparse_sources(child_map, blocks, panel_blocks):
    targets = child_map[:, None, :]
    matches = targets == jnp.arange(blocks, dtype=i32)[None, :, None]
    ids = panel_blocks + jnp.arange(child_map.shape[1], dtype=i32)
    return jnp.sum(jnp.where(matches, ids + 1, 0), axis=2) - 1


def shards(front_tiles, regular, child_map):
    rows = lax.axis_size("row")
    cols = lax.axis_size("col")
    leaves = lax.axis_size("leaf")
    row_at = lax.axis_index("row")
    col_at = lax.axis_index("col")
    side = lax.axis_index("leaf") % 2
    tile = front_tiles.shape[-1]
    outer = front_tiles.shape[1]
    nrows = outer * cols
    ncols = outer * rows
    blocks = nrows * rows
    cap = -(-nrows * ncols * 5 // 256) * 8
    spill = -(-cap // (5 * PART)) * PART
    rooms = (cap,) * 2 + (cap - spill,) * 3 + (spill,) * 3
    width = NPAN * rows * tile // cols
    group = 2
    where = jnp.stack([side, row_at, col_at]).astype(i32)
    flat = front_tiles.reshape(nrows * tile * ncols, tile)
    leaf_pairs = [(i, i ^ 1) for i in range(leaves)]
    col_pairs = [(i, (i - 1) % cols) for i in range(cols)]
    row_pairs = [(i, (i + 1) % rows) for i in range(rows)]
    both_pairs = [
        (i * cols + j, (i ^ 1) * cols + (j - 1) % cols)
        for i in range(leaves)
        for j in range(cols)
    ]

    def from_each_col(value):
        pairs = [[(j, (j - k) % cols) for j in range(cols)] for k in range(cols)]
        return [value] + [lax.ppermute(value, "col", pairs[k]) for k in range(1, cols)]

    own_panel = panel_and_gains(flat, regular.reshape(outer, tile), tile, ncols)
    own_map = child_map.reshape(-1)
    sib_panel = lax.ppermute(own_panel, "leaf", leaf_pairs)
    sib_map = lax.ppermute(own_map, "leaf", leaf_pairs)
    own_panels = from_each_col(own_panel)
    moves = block_moves(own_map, side, row_at, col_at, nrows, ncols, rows, cols)
    entries, counts = block_entries(flat, moves[None], tile, nrows, ncols)
    sib_panel, sib_map, entries, counts = lax.optimization_barrier(
        (sib_panel, sib_map, entries[:1], jnp.minimum(counts[:1], 255.0))
    )
    counts = jnp.maximum(counts, lax.ppermute(counts, "leaf", leaf_pairs))
    mark_row = own_panel.shape[0] - 1
    sib_panel = lax.dynamic_update_slice(sib_panel, counts.astype(bf16), (mark_row, 0))
    sib_panels = from_each_col(sib_panel)
    maps = jnp.stack([own_map, sib_map])
    source = sparse_sources(maps, blocks, NPAN * rows)
    own_panels, entries = lax.optimization_barrier((own_panels, entries))
    found = sorted_blocks(flat, entries, (tile, nrows, ncols, rows, rooms))
    found, own_panels, sib_panels, source = lax.optimization_barrier(
        (found, own_panels, sib_panels, source)
    )
    kept, row_move, col_move, leaf_move, far_move, col_more, leaf_more, far_more = found
    far = lax.ppermute(far_move, ("leaf", "col"), both_pairs)
    beside = lax.ppermute(leaf_move, "leaf", leaf_pairs)
    near = lax.ppermute(col_move, "col", col_pairs)
    across = lax.ppermute(row_move, "row", row_pairs)
    panels = [own_panels, sib_panels]
    panels += [[lax.ppermute(v, "row", row_pairs) for v in kind] for kind in panels]
    inverse, upper = corner_factors(where, panels, tile, ncols, outer)
    factor, left, right, reg = solved_panels(
        source, where, inverse, upper, panels, (tile, nrows, ncols, rows, cols, width)
    )
    marks = jnp.stack([v[mark_row, :5].astype(f32) for v in panels[1] + panels[3]])
    marks = jnp.max(marks, axis=0)
    first_room = cap - spill
    plan = jnp.where(jnp.maximum(marks[2], marks[4]) > first_room, 2, 0)
    plan = plan + jnp.where(marks[3] > first_room, 1, 0)
    over = jnp.max(marks) > cap
    near, beside, far, across, left, right, plan, over = lax.optimization_barrier(
        (near, beside, far, across, left, right, plan, over)
    )

    def rest_of(cols_too, leaves_too):
        def branch(near, beside, far, col_more, leaf_more, far_more):
            if cols_too:
                far_more = lax.ppermute(far_more, ("leaf", "col"), both_pairs)
                col_more = lax.ppermute(col_more, "col", col_pairs)
            if leaves_too:
                leaf_more = lax.ppermute(leaf_more, "leaf", leaf_pairs)
            firsts = [lax.ppermute(v, "row", row_pairs) for v in (near, beside, far)]
            more = [col_more, leaf_more, far_more]
            crossed = [
                lax.ppermute(v, "row", row_pairs) if sent else v
                for v, sent in zip(more, (cols_too, leaves_too, cols_too))
            ]
            return firsts, more, crossed

        return branch

    firsts, more, crossed = lax.switch(
        plan,
        [rest_of(i // 2 == 1, i % 2 == 1) for i in range(4)],
        near, beside, far, col_more, leaf_more, far_more,
    )
    bufs = [kept, across, near, beside, far] + firsts + more + crossed
    owners = (0, 0) + (0, 1, 1) * 4

    def sparse():
        return merged_parent(
            source, where, bufs, owners, reg, left, right,
            (tile, nrows, ncols, rows, cols, group),
        )

    def dense():
        places = jnp.arange(ncols, dtype=i32)
        col_source = source[0][((places // rows) * cols + col_at) * rows + places % rows]
        col_index = jnp.maximum(col_source, 0)
        col_index = col_index // (rows * cols) * rows + col_index % rows
        from_next = (col_source // rows % cols != col_at)[None, :, None, None]
        col_present = (col_source >= 0)[None, :, None, None]
        halves = []
        for half in range(2):
            half_rows = half * (nrows // 2) + jnp.arange(nrows // 2, dtype=i32)
            row_source = source[0][half_rows * rows + row_at]
            start = half * (nrows // 2)
            length = min(nrows // 2 + 1, nrows - start)
            fronts = flat
            if halves:
                fronts, halves[0] = lax.optimization_barrier((flat, halves[0]))
            own = untangled(fronts, tile, ncols, start, length)
            other = lax.ppermute(own, "row", row_pairs)
            row_index = jnp.clip(row_source // rows - start, 0, length - 1)
            is_own = (row_source % rows == row_at)[:, None, None, None]
            picked = jnp.where(
                is_own, jnp.take(own, row_index, axis=0), jnp.take(other, row_index, axis=0)
            )
            picked = jnp.where((row_source >= 0)[:, None, None, None], picked, jnp.zeros_like(picked))
            following = lax.ppermute(picked, "col", col_pairs)
            picked = jnp.where(
                from_next,
                jnp.take(following, col_index, axis=1),
                jnp.take(picked, col_index, axis=1),
            )
            picked = jnp.where(col_present, picked, jnp.zeros_like(picked))
            halves.append(picked.reshape(nrows * ncols // 2, tile, tile))
        stays = jnp.where(side == 0, halves[0], halves[1])
        leaves_here = jnp.where(side == 0, halves[1], halves[0])
        arrived = lax.ppermute(leaves_here, "leaf", leaf_pairs)
        every = nrows * ncols // 2
        part = min(every, tile)
        bufs = []
        for value in (stays, arrived):
            for first in range(0, every, part):
                codes = first + jnp.arange(tile, dtype=i32)
                full = jnp.full((tile,), part, i32)
                listed = jnp.stack([codes // 256, codes % 256, full, full])
                listed = jnp.pad(listed, ((0, tile - 4), (0, 0))).astype(bf16)
                bufs.append(jnp.concatenate([value[first : first + part], listed[None]]))
        owners = (0,) * (len(bufs) // 2) + (1,) * (len(bufs) // 2)
        return merged_parent(
            source, where, bufs, owners, reg, left, right,
            (tile, nrows, ncols, rows, cols, group),
        )

    merged = lax.cond(over, dense, sparse)
    factor = factor.reshape(1, outer, cols, 1, width, tile).swapaxes(4, 5)
    merged = merged.reshape(1, outer // 2, cols, 1, tile, outer, 1, rows, tile)
    return factor, merged


def solution(mesh):
    return jax.shard_map(
        shards,
        mesh=mesh,
        in_specs=(
            P("leaf", None, None, "row", None, None, "col", None, None),
            P("leaf", None, "col", "row", None),
            P("leaf", None),
        ),
        out_specs=(
            P("leaf", None, None, "row", None, "col"),
            P("leaf", None, None, "row", None, None, "col", None, None),
        ),
        check_vma=False,
    )
```

```python
import functools

import jax
import jax.numpy as jnp
from jax import lax
from jax.experimental import pallas as pl
from jax.experimental.pallas import tpu as pltpu
from jax.sharding import PartitionSpec as P

NPAN = 1
VMEM_LIMIT = 60 * 1024 * 1024
PART = 8
f32 = jnp.float32
bf16 = jnp.bfloat16
i32 = jnp.int32
HIGHEST = lax.Precision.HIGHEST


def untangle_kernel(tile, ncols, x_ref, out_ref, wide):
    wide[...] = x_ref[...].astype(f32)
    for j in range(ncols):
        out_ref[j] = wide[pl.ds(j, tile, stride=ncols), :].astype(bf16)


def untangled(x, tile, ncols, start, count):
    return pl.pallas_call(
        functools.partial(untangle_kernel, tile, ncols),
        out_shape=jax.ShapeDtypeStruct((count, ncols, tile, tile), bf16),
        scratch_shapes=[pltpu.VMEM((tile * ncols, tile), f32)],
        grid=(count,),
        in_specs=[pl.BlockSpec((tile * ncols, tile), lambda i: (i + start, 0))],
        out_specs=pl.BlockSpec((None, ncols, tile, tile), lambda i: (i, 0, 0, 0)),
        name="untangle",
    )(x)


def panel_kernel(tile, ncols, outer, x_ref, reg_ref, out_ref, wide):
    wide[...] = x_ref[...].astype(f32)
    for j in range(ncols):
        out_ref[pl.ds(j * tile, tile)] = wide[pl.ds(j, tile, stride=ncols), :].astype(bf16)
    pieces = [piece.astype(f32) for piece in split3(reg_ref[...])]
    pad = out_ref.shape[0] - ncols * tile - 3 * outer
    tail = jnp.concatenate(pieces + [jnp.zeros((pad, tile), f32)], axis=0)
    out_ref[pl.ds(ncols * tile, 3 * outer + pad)] = tail.astype(bf16)


def panel_and_gains(x, reg, tile, ncols):
    outer = reg.shape[0]
    tail = -(-(3 * outer + 1) // 16) * 16
    return pl.pallas_call(
        functools.partial(panel_kernel, tile, ncols, outer),
        out_shape=jax.ShapeDtypeStruct((ncols * tile + tail, tile), bf16),
        scratch_shapes=[pltpu.VMEM((tile * ncols, tile), f32)],
        grid=(1,),
        in_specs=[
            pl.BlockSpec((tile * ncols, tile), lambda i: (0, 0)),
            pl.BlockSpec((outer, tile), lambda i: (0, 0)),
        ],
        out_specs=pl.BlockSpec((ncols * tile + tail, tile), lambda i: (0, 0)),
        name="panel_and_gains",
    )(x, reg)


def flag_kernel(tile, ncols, move_ref, x_ref, entry_ref, count_ref, seen):
    step = pl.program_id(0)
    lines = tile * ncols
    group = x_ref.shape[0] // lines
    for g in range(group):
        x = x_ref[g * lines : (g + 1) * lines]
        at = pl.multiple_of((step * group + g) * ncols, ncols)
        if ncols % 16 == 0:
            top = jnp.max(jnp.abs(x).reshape(tile, ncols, tile), axis=0)
            seen[pl.ds(at, ncols)] = top.astype(f32)
        else:
            top = jnp.max(jnp.abs(x.astype(f32)).reshape(tile, ncols, tile), axis=0)
            for j in range(ncols):
                seen[pl.ds(at + j, 1)] = top[j : j + 1]

    @pl.when(step == pl.num_programs(0) - 1)
    def _():
        along = (((1,), (1,)), ((), ()))
        hits = lax.dot_general(
            jnp.ones((8, tile), f32),
            jnp.where(seen[...] > 0, 1.0, 0.0),
            along,
            preferred_element_type=f32,
        )
        moves = jnp.broadcast_to(move_ref[...], hits.shape)
        entries = jnp.where(hits > 0, moves, -1)
        entry_ref[...] = entries
        kinds = jnp.where(entries[:1] >= 0, entries[:1] & 7, -1)
        ids = lax.broadcasted_iota(i32, (tile, hits.shape[1]), 0)
        count_ref[...] = lax.dot_general(
            jnp.ones(hits.shape, f32),
            jnp.where(ids == kinds, 1.0, 0.0),
            along,
            preferred_element_type=f32,
        )


def block_entries(x, moves, tile, nrows, ncols):
    count = nrows * ncols
    return pl.pallas_call(
        functools.partial(flag_kernel, tile, ncols),
        out_shape=[
            jax.ShapeDtypeStruct((8, count), i32),
            jax.ShapeDtypeStruct((8, tile), f32),
        ],
        grid=(nrows // 8,),
        in_specs=[
            pl.BlockSpec((1, count), lambda i: (0, 0)),
            pl.BlockSpec((8 * tile * ncols, tile), lambda i: (i, 0)),
        ],
        out_specs=[
            pl.BlockSpec((8, count), lambda i: (0, 0)),
            pl.BlockSpec((8, tile), lambda i: (0, 0)),
        ],
        scratch_shapes=[pltpu.VMEM((count, tile), f32)],
        compiler_params=pltpu.CompilerParams(vmem_limit_bytes=VMEM_LIMIT),
        cost_estimate=pl.CostEstimate(flops=0, bytes_accessed=30_000_000, transcendentals=0),
        name="block_entries",
    )(moves, x)


def sort_kernel(dims, entry_ref, x_ref, *rest):
    tile, group, ncols, rows, rooms = dims
    regions = len(rooms)
    bufs = rest[:regions]
    wide, blocks, lists, lists_low, counts, sem = rest[regions:]
    step = pl.program_id(0)
    lines = tile * ncols
    lane = lax.broadcasted_iota(i32, (8, tile), 1)
    sublane = lax.broadcasted_iota(i32, (8, tile), 0)

    @pl.when(step == 0)
    def _():
        lists[...] = jnp.zeros_like(lists)
        for k in range(regions * 2):
            counts[k] = 0

    for g in range(group):
        wide[g] = x_ref[g * lines : (g + 1) * lines].astype(f32)

    def one_row(g, carry):
        for j in range(ncols):
            at = (step * group + g) * ncols + j
            entry = entry_ref[0, at]

            @pl.when(entry >= 0)
            def _():
                kind = entry % 8
                end = entry // 8 % rows
                code = entry // (8 * rows)
                held = counts[kind * 2] + counts[kind * 2 + 1]
                spills = (kind >= 2) & (held >= rooms[2])
                region = jnp.where(spills, kind + 3, kind)
                room = jnp.where(spills, rooms[5], jnp.where(kind >= 2, rooms[2], rooms[0]))
                front = counts[region * 2]
                back = counts[region * 2 + 1]
                slot = jnp.where(end == 0, front, room - 1 - back)

                @pl.when(front + back < room)
                def _():
                    counts[region * 2 + end] = jnp.where(end == 0, front, back) + 1
                    blocks[at] = wide[g, pl.ds(j, tile, stride=ncols), :].astype(bf16)
                    here = jnp.where(sublane == 0, code // 256, code % 256).astype(f32)
                    lists[region] = jnp.where(lane == slot, here, lists[region])
                    for k in range(regions):

                        @pl.when(region == k)
                        def _():
                            pltpu.make_async_copy(blocks.at[at], bufs[k].at[slot], sem).start()

        return carry

    lax.fori_loop(0, group, one_row, 0)

    @pl.when(step == pl.num_programs(0) - 1)
    def _():
        sent = 0
        for k in range(regions):
            front = counts[2 * k]
            back = counts[2 * k + 1]
            sent = sent + front + back
            listed = jnp.where(sublane == 2, front.astype(f32), lists[k])
            listed = jnp.where(sublane == 3, back.astype(f32), listed)
            lists_low[k] = jnp.concatenate([listed, listed], axis=0).astype(bf16)
        copies = [
            pltpu.make_async_copy(lists_low.at[k], bufs[k].at[rooms[k], pl.ds(0, 16)], sem)
            for k in range(regions)
        ]
        for copy in copies:
            copy.start()

        def drain(_, carry):
            pltpu.make_async_copy(blocks.at[0], bufs[0].at[0], sem).wait()
            return carry

        lax.fori_loop(0, sent, drain, 0)
        for copy in copies:
            copy.wait()


def sorted_blocks(x, entries, dims):
    tile, nrows, ncols, rows, rooms = dims
    group = 4
    return pl.pallas_call(
        functools.partial(sort_kernel, (tile, group, ncols, rows, rooms)),
        out_shape=[jax.ShapeDtypeStruct((room + 1, tile, tile), bf16) for room in rooms],
        grid=(nrows // group,),
        in_specs=[
            pl.BlockSpec(memory_space=pltpu.SMEM),
            pl.BlockSpec((group * tile * ncols, tile), lambda i: (i, 0)),
        ],
        out_specs=[pl.BlockSpec(memory_space=pl.ANY)] * len(rooms),
        scratch_shapes=[
            pltpu.VMEM((group, tile * ncols, tile), f32),
            pltpu.VMEM((nrows * ncols, tile, tile), bf16),
            pltpu.VMEM((len(rooms), 8, tile), f32),
            pltpu.VMEM((len(rooms), 16, tile), bf16),
            pltpu.SMEM((len(rooms) * 2,), i32),
            pltpu.SemaphoreType.DMA,
        ],
        compiler_params=pltpu.CompilerParams(vmem_limit_bytes=VMEM_LIMIT),
        cost_estimate=pl.CostEstimate(flops=0, bytes_accessed=60_000_000, transcendentals=0),
        name="sort_blocks",
    )(entries, x)


def block_moves(own_map, side, row_at, col_at, nrows, ncols, rows, cols):
    parent = jnp.concatenate([jnp.full((NPAN * rows,), -1, i32), own_map])
    at_row = parent.reshape(nrows, rows)
    at_row = jnp.where(row_at == 0, at_row[:, 0], at_row[:, 1])[:, None]
    at_col = parent.reshape(nrows // cols, cols, rows)
    at_col = lax.dynamic_index_in_dim(at_col, col_at, 1, keepdims=False).reshape(1, ncols)
    moves_leaf = at_row // (nrows * rows // 2) != side
    moves_col = at_col // rows % cols != col_at
    moves_row = at_row % rows != row_at
    kind = jnp.where(
        moves_leaf,
        jnp.where(moves_col, 4, 3),
        jnp.where(moves_col, 2, jnp.where(moves_row, 1, 0)),
    )
    place_row = at_row // rows % (nrows // 2)
    place_col = at_col // (rows * cols) * rows + at_col % rows
    code = (place_row * ncols + place_col) * rows + at_row % rows
    return jnp.where((at_row >= 0) & (at_col >= 0), code * 8 + kind, -1).reshape(-1)


def eliminate(works, tile):
    rows = lax.broadcasted_iota(i32, (tile, tile), 0)
    lanes = lax.broadcasted_iota(i32, (tile, tile), 1)
    lane_row = lax.broadcasted_iota(i32, (1, tile), 1)

    def one(k, carry):
        values = [work[...] for work in works]
        pivot_rows = [work[pl.ds(k, 1), :] for work in works]
        done = []
        for value, pivot_row in zip(values, pivot_rows):
            column = jnp.sum(jnp.where(lanes == k, value[:, :tile], 0.0), axis=1, keepdims=True)
            pivot = jnp.sum(
                jnp.where(lane_row == k, pivot_row[:, :tile], 0.0), axis=1, keepdims=True
            )
            ratio = jnp.where(rows[:, :1] > k, column, 0.0)
            done.append(value - ratio * (pivot_row * (1.0 / pivot)))
        for work, value in zip(works, done):
            work[...] = value
        return carry

    lax.fori_loop(0, tile, one, 0)


def full_dot(a, b):
    return jnp.dot(a, b, precision=HIGHEST, preferred_element_type=f32)


def corner_kernel(dims, where_ref, *rest):
    tile, ncols, outer, cols = dims
    panels = [rest[kind * cols : (kind + 1) * cols] for kind in range(4)]
    inverse_ref, upper_ref, first_work, second_work, tiles, tails, sem = rest[4 * cols :]
    works = (first_work, second_work)
    row_at = where_ref[1]
    first = lax.rem(cols - where_ref[2], cols)
    tail = tails.shape[2]
    for kind in range(4):
        at = row_at if kind < 2 else 1 - row_at
        leaf = kind % 2

        def copies(ref):
            return (
                pltpu.make_async_copy(ref.at[pl.ds(0, 2 * tile)], tiles.at[at, leaf], sem.at[0, kind]),
                pltpu.make_async_copy(
                    ref.at[pl.ds(ncols * tile, tail)], tails.at[at, leaf], sem.at[1, kind]
                ),
            )

        for k in range(cols):

            @pl.when(first == k)
            def _():
                for copy in copies(panels[kind][k]):
                    copy.start()

    for kind in range(4):
        at = row_at if kind < 2 else 1 - row_at
        pltpu.make_async_copy(
            panels[kind][0].at[pl.ds(0, 2 * tile)], tiles.at[at, kind % 2], sem.at[0, kind]
        ).wait()
        pltpu.make_async_copy(
            panels[kind][0].at[pl.ds(ncols * tile, tail)], tails.at[at, kind % 2], sem.at[1, kind]
        ).wait()
    rows = lax.broadcasted_iota(i32, (tile, tile), 0)
    lanes = lax.broadcasted_iota(i32, (tile, tile), 1)
    eye = jnp.where(rows == lanes, 1.0, 0.0).astype(f32)

    def block(leaf, i, j):
        value = tiles[i, leaf, j * tile : (j + 1) * tile, :].astype(f32)
        if i == j:
            pieces = tails[i, leaf].astype(f32)
            gain = pieces[:1] + pieces[outer : outer + 1] + pieces[2 * outer : 2 * outer + 1]
            value = value + jnp.where(rows == lanes, gain, 0.0)
        return value

    def finish(leaf):
        upper = works[leaf][:, :tile]
        unit = works[leaf][:, tile:]
        pivots = jnp.sum(jnp.where(rows == lanes, upper, 0.0), axis=1, keepdims=True)
        scale = 1.0 / jnp.sqrt(pivots)
        return jnp.where(lanes >= rows, upper * scale, 0.0), jnp.where(
            lanes <= rows, unit * scale, 0.0
        )

    for leaf in range(2):
        works[leaf][:, :tile] = block(leaf, 0, 0)
        works[leaf][:, tile:] = eye
    eliminate(works, tile)
    for leaf in range(2):
        upper, inverse = finish(leaf)
        cross = full_dot(inverse, block(leaf, 0, 1))
        upper_ref[leaf, :tile, :tile] = upper
        upper_ref[leaf, :tile, tile:] = cross
        upper_ref[leaf, tile:, :tile] = jnp.zeros((tile, tile), f32)
        inverse_ref[leaf, :tile, :tile] = inverse
        inverse_ref[leaf, :tile, tile:] = jnp.zeros((tile, tile), f32)
        works[leaf][:, :tile] = block(leaf, 1, 1) - full_dot(cross.T, cross)
        works[leaf][:, tile:] = eye
    eliminate(works, tile)
    for leaf in range(2):
        upper, inverse = finish(leaf)
        cross = upper_ref[leaf, :tile, tile:]
        upper_ref[leaf, tile:, tile:] = upper
        inverse_ref[leaf, tile:, tile:] = inverse
        low = full_dot(cross.T, inverse_ref[leaf, :tile, :tile])
        inverse_ref[leaf, tile:, :tile] = -full_dot(inverse, low)


def corner_factors(where, panels, tile, ncols, outer):
    wide = jax.ShapeDtypeStruct((2, 2 * tile, 2 * tile), f32)
    cols = len(panels[0])
    tail = panels[0][0].shape[0] - ncols * tile
    hbm = pl.BlockSpec(memory_space=pl.ANY)
    vmem = pl.BlockSpec(memory_space=pltpu.VMEM)
    return pl.pallas_call(
        functools.partial(corner_kernel, (tile, ncols, outer, cols)),
        out_shape=[wide, wide],
        in_specs=[pl.BlockSpec(memory_space=pltpu.SMEM)] + [hbm] * (4 * cols),
        out_specs=[vmem, vmem],
        scratch_shapes=[
            pltpu.VMEM((tile, 2 * tile), f32),
            pltpu.VMEM((tile, 2 * tile), f32),
            pltpu.VMEM((2, 2, 2 * tile, tile), bf16),
            pltpu.VMEM((2, 2, tail, tile), bf16),
            pltpu.SemaphoreType.DMA((2, 4)),
        ],
        cost_estimate=pl.CostEstimate(flops=0, bytes_accessed=60_000_000, transcendentals=0),
        name="corner_factors",
    )(where, *[value for kind in panels for value in kind])


def split3(x):
    high = x.astype(bf16)
    rest = x - high.astype(f32)
    mid = rest.astype(bf16)
    low = (rest - mid.astype(f32)).astype(bf16)
    return high, mid, low


def solve_kernel(dims, source_ref, where_ref, inverse_ref, upper_ref, *rest):
    tile, nrows, ncols, rows, cols, width = dims
    given = rest[: 4 * cols]
    factor_ref, left_ref, right_ref, gains_ref, panel, sem = rest[4 * cols :]
    row_at = where_ref[1]
    col_at = where_ref[2]
    outer = ncols // rows
    copies = [
        pltpu.make_async_copy(
            given[kind * cols + k],
            panel.at[row_at if kind < 2 else 1 - row_at, lax.rem(col_at + k, cols), kind % 2],
            sem,
        )
        for kind in range(4)
        for k in range(cols)
    ]
    for copy in copies:
        copy.start()
    for copy in copies:
        copy.wait()
    for s in range(rows):
        for c in range(cols):
            for leaf in range(2):
                pieces = panel[s, c, leaf, ncols * tile :, :].astype(f32)
                gains_ref[(s * cols + c) * 2 + leaf] = (
                    pieces[:outer] + pieces[outer : 2 * outer] + pieces[2 * outer : 3 * outer]
                )
    col_at = where_ref[2]
    half = nrows * rows // 2
    side = where_ref[0]

    def raw(leaf, block):
        at = block // rows % cols
        j = block // (rows * cols) * rows + block % rows
        lines = pl.ds(pl.multiple_of(j * tile, tile), tile)
        return jnp.concatenate([panel[s, at, leaf, lines, :] for s in range(rows)], axis=0)

    def dots(pieces, value):
        total = jnp.dot(pieces[0], value, preferred_element_type=f32)
        for piece in pieces[1:]:
            total = total + jnp.dot(piece, value, preferred_element_type=f32)
        return total

    own = split3(inverse_ref[0, pl.ds(pl.multiple_of(col_at * width, width), width), :])

    def factor(i, carry):
        factor_ref[i] = dots(own, raw(0, i * rows + row_at))
        return carry

    lax.fori_loop(1, nrows, factor, 0, unroll=4)
    top = upper_ref[0, pl.ds(pl.multiple_of(col_at * width, width), width), :]
    factor_ref[0] = jnp.where(row_at == 0, top[:, :tile], top[:, tile:])
    for leaf in range(2):
        pieces = split3(inverse_ref[leaf])

        def solved(block):
            value = dots(pieces, raw(leaf, jnp.maximum(block, 0)))
            return jnp.where(block >= 0, value, 0.0)

        for j in range(ncols):
            parent = ((j // rows) * cols + col_at) * rows + j % rows
            value = solved(source_ref[leaf, parent])
            high = value.astype(bf16)
            low = (value - high.astype(f32)).astype(bf16)
            depth = rows * tile
            lanes = pl.ds(j * tile, tile)
            right_ref[leaf, :depth, lanes] = high
            right_ref[leaf, depth : 2 * depth, lanes] = low
            right_ref[leaf, 2 * depth :, lanes] = high

        def left(i, carry):
            parent = side * half + i * rows + row_at
            value = solved(source_ref[leaf, parent]).T
            high = value.astype(bf16)
            low = (value - high.astype(f32)).astype(bf16)
            left_ref[leaf, i] = jnp.concatenate([high, high, low], axis=1)
            return carry

        lax.fori_loop(0, nrows // 2, left, 0, unroll=4)


def solved_panels(source, where, inverse, upper, panels, dims):
    tile, nrows, ncols, rows, cols, width = dims
    smem = pl.BlockSpec(memory_space=pltpu.SMEM)
    vmem = pl.BlockSpec(memory_space=pltpu.VMEM)
    hbm = pl.BlockSpec(memory_space=pl.ANY)
    depth = 3 * rows * tile
    return pl.pallas_call(
        functools.partial(solve_kernel, dims),
        out_shape=[
            jax.ShapeDtypeStruct((nrows, width, tile), f32),
            jax.ShapeDtypeStruct((2, nrows // 2, tile, depth), bf16),
            jax.ShapeDtypeStruct((2, depth, ncols * tile), bf16),
            jax.ShapeDtypeStruct((rows * cols * 2, ncols // rows, tile), f32),
        ],
        in_specs=[smem, smem, vmem, vmem] + [hbm] * (4 * cols),
        out_specs=[vmem] * 4,
        scratch_shapes=[
            pltpu.VMEM((rows, cols, 2) + panels[0][0].shape, bf16),
            pltpu.SemaphoreType.DMA,
        ],
        compiler_params=pltpu.CompilerParams(vmem_limit_bytes=VMEM_LIMIT),
        cost_estimate=pl.CostEstimate(flops=0, bytes_accessed=1_000_000, transcendentals=0),
        name="solve_panels",
    )(source, where, inverse, upper, *[value for kind in panels for value in kind])


def merge_kernel(dims, leaves, source_ref, where_ref, *rest):
    tile, nrows, ncols, rows, cols, group = dims
    count = len(leaves)
    bufs = rest[:count]
    reg_ref, left_ref, right_ref, out_ref = rest[count : count + 4]
    table, blocks, lists_low, lists_v, lists, sem = rest[count + 4 :]
    step = pl.program_id(0)
    side = where_ref[0]
    row_at = where_ref[1]
    col_at = where_ref[2]
    half = nrows * rows // 2
    per_leaf = nrows // 2 * ncols

    @pl.when(step == 0)
    def _():
        def clear(i, carry):
            table[i] = 0
            return carry

        copies = [
            pltpu.make_async_copy(
                bufs[k].at[bufs[k].shape[0] - 1, pl.ds(0, 16)], lists_low.at[k], sem
            )
            for k in range(count)
        ]
        for copy in copies:
            copy.start()
        lax.fori_loop(0, 2 * per_leaf, clear, 0, unroll=16)
        blocks[0] = jnp.zeros((tile, tile), bf16)
        for copy in copies:
            copy.wait()
        for k in range(count):
            listed = lists_low[k].astype(f32)
            codes = listed[0:1] * 256.0 + listed[1:2]
            lists_v[k] = jnp.concatenate([codes, listed[2:4]] + [codes] * 5, axis=0).astype(i32)
        copy = pltpu.make_async_copy(lists_v, lists, sem)
        copy.start()
        copy.wait()
        base = 1
        started = 0
        for k in range(count):
            room = bufs[k].shape[0] - 1
            mine = lists[k, 1 + row_at, 0]
            first = jnp.where(row_at == 0, 0, room - mine)
            parts = lax.div(mine + (PART - 1), PART)

            def fetch(c, carry):
                at = jnp.where(row_at == 0, c * PART, room - PART - c * PART)
                pltpu.make_async_copy(
                    bufs[k].at[pl.ds(at, PART)], blocks.at[pl.ds(base + at, PART)], sem
                ).start()
                return carry

            lax.fori_loop(0, parts, fetch, 0)

            def place(e, carry):
                table[leaves[k] * per_leaf + lists[k, 0, e]] = base + e
                return carry

            lax.fori_loop(first, first + mine, place, 0)
            base = base + room
            started = started + parts

        def drain(_, carry):
            pltpu.make_async_copy(
                bufs[0].at[pl.ds(0, PART)], blocks.at[pl.ds(1, PART)], sem
            ).wait()
            return carry

        lax.fori_loop(0, started, drain, 0)

    def less(slot, update):
        return (blocks[slot].astype(f32) - update).astype(bf16).astype(f32)

    wide = min(2, ncols)
    lefts = [left_ref[leaf].reshape(group * tile, left_ref.shape[-1]) for leaf in range(2)]
    for first in range(0, ncols, wide):
        updates = [
            jnp.dot(
                lefts[leaf],
                right_ref[leaf, :, first * tile : (first + wide) * tile],
                preferred_element_type=f32,
            )
            for leaf in range(2)
        ]
        for g in range(group):
            for w in range(wide):
                j = first + w
                parts = []
                for leaf in range(2):
                    slot = table[leaf * per_leaf + (step * group + g) * ncols + j]
                    update = updates[leaf][g * tile : (g + 1) * tile, w * tile : (w + 1) * tile]
                    parts.append(less(slot, update))
                out_ref[pl.ds(g * tile * ncols + j, tile, stride=ncols), :] = parts[0] + parts[1]

    on_diagonal = lax.broadcasted_iota(i32, (tile, tile), 0) == lax.broadcasted_iota(
        i32, (tile, tile), 1
    )
    for g in range(group):
        place_row = step * group + g
        parent = side * half + place_row * rows + row_at

        @pl.when(parent // rows % cols == col_at)
        def _():
            j = parent // (rows * cols) * rows + parent % rows
            parts = []
            for leaf in range(2):
                block = source_ref[leaf, parent]
                present = jnp.maximum(block, 0)
                at = (present % rows * cols + present // rows % cols) * 2 + leaf
                gain = reg_ref[at, pl.ds(present // (rows * cols), 1), :]
                gain = jnp.where(on_diagonal & (block >= 0), gain, 0.0)
                update = jnp.dot(
                    left_ref[leaf, g],
                    right_ref[leaf, :, pl.ds(pl.multiple_of(j * tile, tile), tile)],
                    preferred_element_type=f32,
                )
                parts.append(less(table[leaf * per_leaf + place_row * ncols + j], update - gain))
            out_ref[pl.ds(g * tile * ncols + j, tile, stride=ncols), :] = parts[0] + parts[1]


def merged_parent(source, where, bufs, leaves, reg, left, right, dims):
    tile, nrows, ncols, rows, cols, group = dims
    count = len(leaves)
    smem = pl.BlockSpec(memory_space=pltpu.SMEM)
    hbm = pl.BlockSpec(memory_space=pl.ANY)
    vmem = pl.BlockSpec(memory_space=pltpu.VMEM)
    depth = left.shape[-1]
    return pl.pallas_call(
        functools.partial(merge_kernel, dims, leaves),
        out_shape=jax.ShapeDtypeStruct((nrows // 2 * tile * ncols, tile), f32),
        grid=(nrows // 2 // group,),
        in_specs=[smem] * 2
        + [hbm] * count
        + [
            vmem,
            pl.BlockSpec((2, group, tile, depth), lambda i: (0, i, 0, 0)),
            vmem,
        ],
        out_specs=pl.BlockSpec((group * tile * ncols, tile), lambda i: (i, 0)),
        scratch_shapes=[
            pltpu.SMEM((nrows * ncols,), i32),
            pltpu.VMEM((1 + sum(buf.shape[0] - 1 for buf in bufs), tile, tile), bf16),
            pltpu.VMEM((count, 16, tile), bf16),
            pltpu.VMEM((count, 8, tile), i32),
            pltpu.SMEM((count, 8, tile), i32),
            pltpu.SemaphoreType.DMA,
        ],
        compiler_params=pltpu.CompilerParams(vmem_limit_bytes=VMEM_LIMIT),
        name="merge_parent",
    )(source, where, *bufs, reg, left, right)


def sparse_sources(child_map, blocks, panel_blocks):
    targets = child_map[:, None, :]
    matches = targets == jnp.arange(blocks, dtype=i32)[None, :, None]
    ids = panel_blocks + jnp.arange(child_map.shape[1], dtype=i32)
    return jnp.sum(jnp.where(matches, ids + 1, 0), axis=2) - 1


def shards(front_tiles, regular, child_map):
    rows = lax.axis_size("row")
    cols = lax.axis_size("col")
    leaves = lax.axis_size("leaf")
    row_at = lax.axis_index("row")
    col_at = lax.axis_index("col")
    side = lax.axis_index("leaf") % 2
    tile = front_tiles.shape[-1]
    outer = front_tiles.shape[1]
    nrows = outer * cols
    ncols = outer * rows
    blocks = nrows * rows
    cap = -(-nrows * ncols * 5 // 256) * 8
    spill = -(-cap // (5 * PART)) * PART
    rooms = (cap,) * 2 + (cap - spill,) * 3 + (spill,) * 3
    width = NPAN * rows * tile // cols
    group = 2
    where = jnp.stack([side, row_at, col_at]).astype(i32)
    flat = front_tiles.reshape(nrows * tile * ncols, tile)
    leaf_pairs = [(i, i ^ 1) for i in range(leaves)]
    col_pairs = [(i, (i - 1) % cols) for i in range(cols)]
    row_pairs = [(i, (i + 1) % rows) for i in range(rows)]
    both_pairs = [
        (i * cols + j, (i ^ 1) * cols + (j - 1) % cols)
        for i in range(leaves)
        for j in range(cols)
    ]

    def from_each_col(value):
        pairs = [[(j, (j - k) % cols) for j in range(cols)] for k in range(cols)]
        return [value] + [lax.ppermute(value, "col", pairs[k]) for k in range(1, cols)]

    own_panel = panel_and_gains(flat, regular.reshape(outer, tile), tile, ncols)
    own_map = child_map.reshape(-1)
    sib_panel = lax.ppermute(own_panel, "leaf", leaf_pairs)
    sib_map = lax.ppermute(own_map, "leaf", leaf_pairs)
    own_panels = from_each_col(own_panel)
    moves = block_moves(own_map, side, row_at, col_at, nrows, ncols, rows, cols)
    entries, counts = block_entries(flat, moves[None], tile, nrows, ncols)
    sib_panel, sib_map, entries, counts = lax.optimization_barrier(
        (sib_panel, sib_map, entries[:1], jnp.minimum(counts[:1], 255.0))
    )
    counts = jnp.maximum(counts, lax.ppermute(counts, "leaf", leaf_pairs))
    mark_row = own_panel.shape[0] - 1
    sib_panel = lax.dynamic_update_slice(sib_panel, counts.astype(bf16), (mark_row, 0))
    sib_panels = from_each_col(sib_panel)
    maps = jnp.stack([own_map, sib_map])
    source = sparse_sources(maps, blocks, NPAN * rows)
    own_panels, entries = lax.optimization_barrier((own_panels, entries))
    found = sorted_blocks(flat, entries, (tile, nrows, ncols, rows, rooms))
    found, own_panels, sib_panels, source = lax.optimization_barrier(
        (found, own_panels, sib_panels, source)
    )
    kept, row_move, col_move, leaf_move, far_move, col_more, leaf_more, far_more = found
    far = lax.ppermute(far_move, ("leaf", "col"), both_pairs)
    beside = lax.ppermute(leaf_move, "leaf", leaf_pairs)
    near = lax.ppermute(col_move, "col", col_pairs)
    across = lax.ppermute(row_move, "row", row_pairs)
    panels = [own_panels, sib_panels]
    panels += [[lax.ppermute(v, "row", row_pairs) for v in kind] for kind in panels]
    inverse, upper = corner_factors(where, panels, tile, ncols, outer)
    factor, left, right, reg = solved_panels(
        source, where, inverse, upper, panels, (tile, nrows, ncols, rows, cols, width)
    )
    marks = jnp.stack([v[mark_row, :5].astype(f32) for v in panels[1] + panels[3]])
    marks = jnp.max(marks, axis=0)
    first_room = cap - spill
    plan = jnp.where(jnp.maximum(marks[2], marks[4]) > first_room, 2, 0)
    plan = plan + jnp.where(marks[3] > first_room, 1, 0)
    over = jnp.max(marks) > cap
    near, beside, left, right = lax.optimization_barrier((near, beside, left, right))
    firsts = [lax.ppermute(v, "row", row_pairs) for v in (near, beside)]
    firsts, far, across, left, right, plan, over = lax.optimization_barrier(
        (firsts, far, across, left, right, plan, over)
    )

    def rest_of(cols_too, leaves_too):
        def branch(far, col_more, leaf_more, far_more):
            if cols_too:
                far_more = lax.ppermute(far_more, ("leaf", "col"), both_pairs)
                col_more = lax.ppermute(col_more, "col", col_pairs)
            if leaves_too:
                leaf_more = lax.ppermute(leaf_more, "leaf", leaf_pairs)
            last = lax.ppermute(far, "row", row_pairs)
            more = [col_more, leaf_more, far_more]
            crossed = [
                lax.ppermute(v, "row", row_pairs) if sent else v
                for v, sent in zip(more, (cols_too, leaves_too, cols_too))
            ]
            return last, more, crossed

        return branch

    last, more, crossed = lax.switch(
        plan,
        [rest_of(i // 2 == 1, i % 2 == 1) for i in range(4)],
        far, col_more, leaf_more, far_more,
    )
    bufs = [kept, across, near, beside, far] + firsts + [last] + more + crossed
    owners = (0, 0) + (0, 1, 1) * 4

    def sparse():
        return merged_parent(
            source, where, bufs, owners, reg, left, right,
            (tile, nrows, ncols, rows, cols, group),
        )

    def dense():
        places = jnp.arange(ncols, dtype=i32)
        col_source = source[0][((places // rows) * cols + col_at) * rows + places % rows]
        col_index = jnp.maximum(col_source, 0)
        col_index = col_index // (rows * cols) * rows + col_index % rows
        from_next = (col_source // rows % cols != col_at)[None, :, None, None]
        col_present = (col_source >= 0)[None, :, None, None]
        halves = []
        for half in range(2):
            half_rows = half * (nrows // 2) + jnp.arange(nrows // 2, dtype=i32)
            row_source = source[0][half_rows * rows + row_at]
            start = half * (nrows // 2)
            length = min(nrows // 2 + 1, nrows - start)
            fronts = flat
            if halves:
                fronts, halves[0] = lax.optimization_barrier((flat, halves[0]))
            own = untangled(fronts, tile, ncols, start, length)
            other = lax.ppermute(own, "row", row_pairs)
            row_index = jnp.clip(row_source // rows - start, 0, length - 1)
            is_own = (row_source % rows == row_at)[:, None, None, None]
            picked = jnp.where(
                is_own, jnp.take(own, row_index, axis=0), jnp.take(other, row_index, axis=0)
            )
            picked = jnp.where((row_source >= 0)[:, None, None, None], picked, jnp.zeros_like(picked))
            following = lax.ppermute(picked, "col", col_pairs)
            picked = jnp.where(
                from_next,
                jnp.take(following, col_index, axis=1),
                jnp.take(picked, col_index, axis=1),
            )
            picked = jnp.where(col_present, picked, jnp.zeros_like(picked))
            halves.append(picked.reshape(nrows * ncols // 2, tile, tile))
        stays = jnp.where(side == 0, halves[0], halves[1])
        leaves_here = jnp.where(side == 0, halves[1], halves[0])
        arrived = lax.ppermute(leaves_here, "leaf", leaf_pairs)
        every = nrows * ncols // 2
        part = min(every, tile)
        bufs = []
        for value in (stays, arrived):
            for first in range(0, every, part):
                codes = first + jnp.arange(tile, dtype=i32)
                full = jnp.full((tile,), part, i32)
                listed = jnp.stack([codes // 256, codes % 256, full, full])
                listed = jnp.pad(listed, ((0, tile - 4), (0, 0))).astype(bf16)
                bufs.append(jnp.concatenate([value[first : first + part], listed[None]]))
        owners = (0,) * (len(bufs) // 2) + (1,) * (len(bufs) // 2)
        return merged_parent(
            source, where, bufs, owners, reg, left, right,
            (tile, nrows, ncols, rows, cols, group),
        )

    merged = lax.cond(over, dense, sparse)
    factor = factor.reshape(1, outer, cols, 1, width, tile).swapaxes(4, 5)
    merged = merged.reshape(1, outer // 2, cols, 1, tile, outer, 1, rows, tile)
    return factor, merged


def solution(mesh):
    return jax.shard_map(
        shards,
        mesh=mesh,
        in_specs=(
            P("leaf", None, None, "row", None, None, "col", None, None),
            P("leaf", None, "col", "row", None),
            P("leaf", None),
        ),
        out_specs=(
            P("leaf", None, None, "row", None, "col"),
            P("leaf", None, None, "row", None, None, "col", None, None),
        ),
        check_vma=False,
    )
```
